256 devices in a mesh: fsdp: 32 (over y, z), tensor: 8 (over x, core).
Axes of the slice: x: 4, y: 4, z: 8, core: 2. Of those that a mesh axis runs over, the one named last changes fastest.
Arguments:
- momentum: float32 [28672, 8192], P('fsdp', 'tensor'), may hold values from -150 to 150
- gradient: bfloat16 [28672, 8192], P('fsdp', 'tensor'), may hold values from -6 to 6
- basis: bfloat16 [8192, 512], P('tensor'), may hold values from -0.0625 to 0.0625
Outputs:
- new_momentum: float32 [28672, 8192], P('fsdp', 'tensor')
- left_factor: float32 [28672, 512], P(('fsdp', 'tensor'))
- new_basis: bfloat16 [8192, 512], P('tensor')
The draws below stay inside these ranges and needn't reach their ends.
All inputs are finite; a program needn't handle non-finite values.
Results may differ from the reference program's by a relative error of at most 0.001.
Values sent between devices are 32-bit elements; how exact they have to be, the bound alone decides.
A program may use at most 128 MiB of HBM per device.

```python
import math
import jax
import jax.numpy as jnp
from jax import lax

FF = 28672
D = 8192
RANK = 512


def draw_momentum(key, part):
    key = jax.random.fold_in(key, 11)
    keys = jax.random.split(key, 3)
    row_pos = jnp.arange(FF, dtype=jnp.float32) / FF
    col_pos = jnp.arange(D, dtype=jnp.float32) / D
    row_scale = jnp.exp(math.log(3.0) * row_pos + jax.random.uniform(keys[0], (FF,), jnp.float32, 0.0, math.log(10.0))) / 6.0
    col_scale = jnp.exp(math.log(3.0) * col_pos + jax.random.uniform(keys[1], (D,), jnp.float32, 0.0, math.log(10.0))) / 6.0
    noise = jnp.clip(jax.random.normal(keys[2], (FF, D), jnp.float32), -6.0, 6.0)
    return (noise * row_scale[:, None] * col_scale[None, :]).astype(jnp.float32)


def level_of(stream_key, dims, cuts, low, largest):
    factor_of = 1.0
    for position, blocks in cuts:
        heights = jax.random.uniform(jax.random.fold_in(jax.random.fold_in(stream_key, 6), position), (blocks,), jnp.float32, low / len(cuts), largest / len(cuts))
        factor_of = factor_of * jnp.repeat(jnp.exp(heights), dims[position] // blocks).reshape((-1,) + (1,) * (len(dims) - 1 - position))
    return factor_of


def gaussian(key, extent, spread, most, pieces=(), kind=jnp.bfloat16):
    factor_of = level_of(key, extent, pieces, -0.22, 0.18) if pieces else 1.0
    result = jax.random.normal(key, extent, jnp.float32) * spread * factor_of
    return jnp.minimum(jnp.maximum(result, -most), most).astype(kind)


def setup_inputs(seed: int = 0) -> dict:
    splits = jax.random.split(jax.random.key(seed), 4)
    momentum = draw_momentum(jax.random.fold_in(splits[3], 71), 0)
    gradient = gaussian(splits[1], (FF, D), 1.0, 6.0, ((0, 32), (1, 8)))
    basis = gaussian(splits[2], (D, RANK), D ** -0.5, 0.0625, ((0, 8),))
    return dict(momentum=momentum, gradient=gradient, basis=basis)


precise = lax.Precision.HIGHEST
mu_value = 0.95
eps_value = 1e-06

def reference(momentum, gradient, basis):
    basis_wide = basis.astype(jnp.float32)
    block_rows = math.gcd(FF, 1024)
    block_count = FF // block_rows
    mom_blocks = momentum.reshape(block_count, block_rows, D)
    grad_blocks = gradient.reshape(block_count, block_rows, D)

    def project(blocks_in):
        blended = blocks_in[0] + blocks_in[1].astype(jnp.float32)
        return jnp.dot(blended.astype(jnp.float32), basis_wide.astype(jnp.float32), precision=precise, preferred_element_type=jnp.float32)
    projected = lax.map(project, (mom_blocks, grad_blocks)).reshape(FF, RANK)
    gram = jnp.dot(projected.T.astype(jnp.float32), projected.astype(jnp.float32), precision=precise, preferred_element_type=jnp.float32)
    factor_low = jnp.linalg.cholesky(gram)
    left_factor = lax.linalg.triangular_solve(factor_low, projected, left_side=False, lower=True, transpose_a=True)
    left_blocks = left_factor.reshape(block_count, block_rows, RANK)

    def accumulate(carry, blocks_in):
        blended = blocks_in[0] + blocks_in[1].astype(jnp.float32)
        return (carry + jnp.dot(blended.T.astype(jnp.float32), blocks_in[2].astype(jnp.float32), precision=precise, preferred_element_type=jnp.float32), None)
    coefficients, unused = lax.scan(accumulate, jnp.zeros((D, RANK), jnp.float32), (mom_blocks, grad_blocks, left_blocks))
    column_norm = jnp.sqrt(lax.optimization_barrier(jnp.sum(coefficients * coefficients, axis=0)) + eps_value)
    new_basis = (coefficients / column_norm[None, :]).astype(jnp.bfloat16)

    def correct(blocks_in):
        blended = blocks_in[0] + blocks_in[1].astype(jnp.float32)
        return blended - (1.0 - mu_value) * jnp.dot(blocks_in[2].astype(jnp.float32), coefficients.T.astype(jnp.float32), precision=precise, preferred_element_type=jnp.float32)
    new_momentum = lax.map(correct, (mom_blocks, grad_blocks, left_blocks)).reshape(FF, D)
    return (new_momentum, left_factor, new_basis)
```

```python
import functools

import jax
import jax.numpy as jnp
from jax import lax
from jax.experimental import pallas as pl
from jax.experimental.pallas import tpu as pltpu
from jax.sharding import PartitionSpec as P

mu_value = 0.95
eps_value = 1e-06
f32 = jnp.float32
bf16 = jnp.bfloat16
MESH = pl.DeviceIdType.MESH
HIGHEST = lax.Precision.HIGHEST
NB = 128


def dot(left, right, dims=((1,), (0,)), precision=None):
    return lax.dot_general(left, right, (dims, ((), ())), precision=precision, preferred_element_type=f32)


def exact_dot(left, right, dims=((1,), (0,))):
    return dot(left, right, dims, HIGHEST)


def split2(value):
    high = value.astype(bf16)
    return high, (value - high.astype(f32)).astype(bf16)


def dot3(left, right, dims=((1,), (0,))):
    left_high, left_low = left
    right_high, right_low = right
    return dot(left_high, right_high, dims) + (dot(left_low, right_high, dims) + dot(left_high, right_low, dims))


def factor_groups(work, inverse, first, last):
    for group in range(first, last):
        r0 = 8 * group
        n = NB - r0
        cols = [jnp.broadcast_to(work[r0:NB, r0 + j : r0 + j + 1], (n, 128)) for j in range(8)]
        top = work[r0 : r0 + 8, :]
        rows = []
        for k in range(8):
            inv = lax.rsqrt(cols[k][k : k + 1, :])
            c = cols[k] * inv
            cols[k] = c
            for j in range(k + 1, 8):
                cols[j] = cols[j] - c * c[j : j + 1, :]
            row = top[k : k + 1, :] * jnp.concatenate([inv, inv], axis=1)
            rows.append(row)
            if k < 7:
                top = top - jnp.concatenate([c[0:8], c[0:8]], axis=1) * row
            inverse[r0 + k : r0 + k + 1, :] = row[:, 128:]
        if n > 8:
            for half in (slice(0, 128), slice(128, 256)):
                rest = work[r0 + 8 : NB, half]
                for k in range(8):
                    rest = rest - cols[k][8:] * rows[k][:, half]
                work[r0 + 8 : NB, half] = rest


class Links:
    def __init__(self, dims, send_sems, recv_sems):
        self.nx, self.ny, self.nz = dims
        f, t = lax.axis_index("fsdp"), lax.axis_index("tensor")
        self.y, self.z = f // self.nz, lax.rem(f, self.nz)
        self.x, self.c = t // 2, lax.rem(t, 2)
        self.t, self.f = t, f
        self.send_sems, self.recv_sems = send_sems, recv_sems
        self.count = 0
        self.sent = []

    def size(self, axis):
        return {"x": self.nx, "y": self.ny, "z": self.nz}[axis]

    def pos(self, axis):
        return {"x": self.x, "y": self.y, "z": self.z}[axis]

    def at(self, axis, offset):
        n = self.size(axis)
        return lax.rem(self.pos(axis) + (offset % n), n)

    def device(self, dx=0, dy=0, dz=0, core=0):
        x, y, z = self.at("x", dx), self.at("y", dy), self.at("z", dz)
        c = 1 - self.c if core else self.c
        return (y * self.nz + z, x * 2 + c)

    def along(self, axis, offset):
        return self.device(**{"d" + axis: offset})

    def send(self, src, dst, device):
        number = self.count
        self.count += 1
        copy = pltpu.make_async_remote_copy(
            src_ref=src,
            dst_ref=dst,
            send_sem=self.send_sems.at[number],
            recv_sem=self.recv_sems.at[number],
            device_id=device,
            device_id_type=MESH,
        )
        copy.start()
        self.sent.append(copy)
        return number

    def wait(self, number, landing):
        pltpu.make_async_remote_copy(
            src_ref=landing,
            dst_ref=landing,
            send_sem=self.send_sems.at[number],
            recv_sem=self.recv_sems.at[number],
            device_id=self.device(core=1),
            device_id_type=MESH,
        ).wait_recv()


def halves(width):
    return (slice(0, width // 2), slice(width // 2, width))


def reduce_ring(links, axis, block, plus, minus, width):
    n = links.size(axis)
    half = n // 2
    first, second = halves(width)
    state = {}

    def add(target, slot, cols):
        target[:, cols] = target[:, cols] + slot[:, cols]

    def step(s):
        k = half + 1 - s
        ahead, behind = block(links.at(axis, k)), block(links.at(axis, -k))
        if s > 1:
            cols_a = first if s == 2 else slice(0, width)
            cols_b = second if s == 2 else slice(0, width)
            links.wait(state["plus"], plus.at[s - 2, :, cols_a])
            add(ahead, plus.at[s - 2], cols_a)
        cols_a = first if s == 1 else slice(0, width)
        state["plus"] = links.send(ahead.at[:, cols_a], plus.at[s - 1, :, cols_a], links.along(axis, 1))
        if s > 1:
            links.wait(state["minus"], minus.at[s - 2, :, cols_b])
            add(behind, minus.at[s - 2], cols_b)
        cols_b = second if s == 1 else slice(0, width)
        state["minus"] = links.send(behind.at[:, cols_b], minus.at[s - 1, :, cols_b], links.along(axis, -1))

    def last():
        own = block(links.pos(axis))
        cols_a = first if half == 1 else slice(0, width)
        cols_b = second if half == 1 else slice(0, width)
        links.wait(state["plus"], plus.at[half - 1, :, cols_a])
        add(own, plus.at[half - 1], cols_a)
        links.wait(state["minus"], minus.at[half - 1, :, cols_b])
        add(own, minus.at[half - 1], cols_b)

    return [functools.partial(step, s) for s in range(1, half + 1)] + [last]


def gather_ring(links, axis, block, cut, on_block=None):
    n = links.size(axis)
    half = n // 2
    state = {}

    def step(s):
        ahead, behind = block(links.at(axis, 1 - s)), block(links.at(axis, s - 1))
        if s > 1:
            links.wait(state["plus"], ahead)
        view = cut(ahead)[0] if s == half else ahead
        state["plus"] = links.send(view, view, links.along(axis, 1))
        if s > 1:
            links.wait(state["minus"], behind)
        view = cut(behind)[1] if s == half else behind
        state["minus"] = links.send(view, view, links.along(axis, -1))
        if on_block is not None:
            on_block(links.at(axis, 1 - s))
            if s > 1:
                on_block(links.at(axis, s - 1))

    def last():
        far = cut(block(links.at(axis, half)))
        links.wait(state["plus"], far[0])
        links.wait(state["minus"], far[1])
        if on_block is not None:
            on_block(links.at(axis, half))

    return [functools.partial(step, s) for s in range(1, half + 1)] + [last]


def cut_columns(view):
    width = view.shape[1]
    return view.at[:, 0 : width // 2], view.at[:, width // 2 : width]


def cut_rows(view):
    size = view.shape[0]
    return view.at[0 : size // 2], view.at[size // 2 : size]


def kernel(
    dims,
    mom_hbm, grad_hbm, basis_hbm,
    out_hbm, left_hbm, newb_hbm,
    blend, grad, basis, blend_hi, blend_lo, part, from_core, x_plus, x_minus,
    full, flip, flip_hi, flip_lo,
    piece, from_y, from_z, tiles, gram_all, sym, low, work, diag_inv, inverse,
    wide, ay_plus, ay_minus, az_plus, az_minus, bz_plus, bz_minus, by_plus, by_minus, wide_all,
    coef_t, coef, squares, left_bf, left_own, newb,
    load_sems, store_sems, send_sems, recv_sems,
):
    nx, ny, nz = dims
    nt = 2 * nx
    rows, width = blend.shape
    rank = basis.shape[1]
    share = rows // nt
    links = Links(dims, send_sems, recv_sems)
    chip_rows = 2 * share

    loads = []
    basis_copy = pltpu.make_async_copy(basis_hbm, basis, load_sems.at[2 * nx])
    basis_copy.start()
    for k in range(nx):
        chip = links.at("x", [nx // 2, 1, nx - 1, 0][k] if nx == 4 else k + 1)
        span = pl.ds(pl.multiple_of(chip * chip_rows, chip_rows), chip_rows)
        m = pltpu.make_async_copy(mom_hbm.at[span], blend.at[span], load_sems.at[2 * k])
        g = pltpu.make_async_copy(grad_hbm.at[span], grad.at[span], load_sems.at[2 * k + 1])
        m.start()
        g.start()
        loads.append((m, g, span, chip))

    barrier = pltpu.get_barrier_semaphore()
    peers = [links.device(core=1)]
    peers += [links.device(dx=d, core=c) for d in range(1, nx) for c in (0, 1)]
    peers += [links.along("y", d) for d in range(1, ny)]
    peers += [links.along("z", d) for d in range(1, nz)]
    for peer in peers:
        pl.semaphore_signal(barrier, inc=1, device_id=peer, device_id_type=MESH)
    pl.semaphore_wait(barrier, len(peers))

    def share_of(ref, chip, core):
        return ref.at[pl.ds(pl.multiple_of((2 * chip + core) * share, share), share)]

    basis_copy.wait()
    core_numbers = []
    for m, g, span, chip in loads:
        m.wait()
        g.wait()
        value = blend[span] + grad[span].astype(f32)
        blend[span] = value
        high = value.astype(bf16)
        rest = value - high.astype(f32)
        mid = rest.astype(bf16)
        tail = (rest - mid.astype(f32)).astype(bf16)
        blend_hi[span] = high
        blend_lo[span] = mid
        q = basis[...]
        part[span] = dot(high, q) + (dot(mid, q) + dot(tail, q))
        number = links.send(
            share_of(part, chip, 1 - links.c), from_core.at[pl.ds(chip * share, share)], links.device(core=1)
        )
        core_numbers.append((number, chip))
    for number, chip in core_numbers:
        landing = from_core.at[pl.ds(chip * share, share)]
        links.wait(number, landing)
        mine = share_of(part, chip, links.c)
        mine[...] = mine[...] + landing[...]

    for step in reduce_ring(links, "x", lambda i: share_of(part, i, links.c), x_plus, x_minus, rank):
        step()
    own = share_of(part, links.x, links.c)
    share_of(full, links.x, links.c)[...] = own[...]

    def gather_tensor(view, cut):
        numbers = []

        def to_core(chip):
            numbers.append((links.send(view(chip, links.c), view(chip, links.c), links.device(core=1)), chip))

        def finish():
            for number, chip in numbers:
                links.wait(number, view(chip, 1 - links.c))

        return gather_ring(links, "x", lambda i: view(i, links.c), cut, to_core) + [finish]

    for step in gather_tensor(functools.partial(share_of, full), cut_columns):
        step()

    for i in range(rows // 128):
        for j in range(rank // 128):
            block = full[128 * i : 128 * i + 128, 128 * j : 128 * j + 128].T
            flip[128 * j : 128 * j + 128, 128 * i : 128 * i + 128] = block
            high, lower = split2(block)
            flip_hi[128 * j : 128 * j + 128, 128 * i : 128 * i + 128] = high
            flip_lo[128 * j : 128 * j + 128, 128 * i : 128 * i + 128] = lower

    nb = rank // NB
    fine = NB // nt
    picked = jnp.concatenate(
        [flip[pl.ds(pl.multiple_of(NB * i + fine * links.t, 8), fine), :] for i in range(nb)], axis=0
    )
    strip = exact_dot(picked, full[...])
    blocks = [(i, j) for i in range(nb) for j in range(i, nb)]
    per = fine // 8
    for b, (i, j) in enumerate(blocks):
        piece[b * fine : b * fine + fine, :] = strip[i * fine : i * fine + fine, NB * j : NB * j + NB]
    piece_rows = len(blocks) * fine
    y_rows = piece_rows // ny

    def y_view(ref, i):
        return ref.at[pl.ds(pl.multiple_of(i * y_rows, 8), y_rows)]

    y_numbers = [
        links.send(y_view(piece, links.at("y", d)), from_y.at[d - 1], links.along("y", d)) for d in range(1, ny)
    ]

    def wide_part(h):
        span = slice(h * (rank // 2), (h + 1) * (rank // 2))
        for j in range(width // 256):
            cols = slice(256 * j, 256 * j + 256)
            wide[span, cols] = dot3((flip_hi[span, :], flip_lo[span, :]), (blend_hi[:, cols], blend_lo[:, cols]))

    wide_part(0)
    total = y_view(piece, links.y)[...]
    for d, number in zip(range(1, ny), y_numbers):
        links.wait(number, from_y.at[d - 1])
        total = total + from_y[d - 1]
    from_z[links.z] = total
    z_numbers = [
        links.send(from_z.at[links.z], from_z.at[links.z], links.along("z", d)) for d in range(1, nz)
    ]
    wide_part(1)
    for d, number in zip(range(1, nz), z_numbers):
        links.wait(number, from_z.at[links.at("z", -d)])
    total = from_z[0]
    for i in range(1, nz):
        total = total + from_z[i]
    mine = gram_all.at[links.t]
    y_view(mine, links.y)[...] = total
    y_numbers = [
        links.send(y_view(mine, links.y), y_view(mine, links.y), links.along("y", d)) for d in range(1, ny)
    ]

    half = rank // 2
    ay, az = half // ny, half // ny // nz
    bz, by = half // nz, half // nz // ny
    start_az = links.y * ay
    start_bz = half + links.z * bz

    def rows_of(ref, start, size):
        return ref.at[pl.ds(pl.multiple_of(start, 8), size)]

    def copy_out_a():
        rows_of(wide_all, start_az + links.z * az, az)[...] = rows_of(wide, start_az + links.z * az, az)[...]

    def copy_out_b():
        rows_of(wide_all, start_bz + links.y * by, by)[...] = rows_of(wide, start_bz + links.y * by, by)[...]

    hooks_a = (
        reduce_ring(links, "y", lambda i: rows_of(wide, i * ay, ay), ay_plus, ay_minus, width)
        + reduce_ring(links, "z", lambda i: rows_of(wide, start_az + i * az, az), az_plus, az_minus, width)
        + [copy_out_a]
        + gather_ring(links, "z", lambda i: rows_of(wide_all, start_az + i * az, az), cut_columns)
        + gather_ring(links, "y", lambda i: rows_of(wide_all, i * ay, ay), cut_columns)
    )
    hooks_b = (
        reduce_ring(links, "z", lambda i: rows_of(wide, half + i * bz, bz), bz_plus, bz_minus, width)
        + reduce_ring(links, "y", lambda i: rows_of(wide, start_bz + i * by, by), by_plus, by_minus, width)
        + [copy_out_b]
        + gather_ring(links, "y", lambda i: rows_of(wide_all, start_bz + i * by, by), cut_columns)
        + gather_ring(links, "z", lambda i: rows_of(wide_all, half + i * bz, bz), cut_columns)
    )
    hooks = []
    for a, b in zip(hooks_a, hooks_b):
        hooks += [b, a]
    assert len(hooks_a) == len(hooks_b)
    hooks.reverse()

    def serve(count):
        for _ in range(count):
            if hooks:
                hooks.pop()()

    for d, number in zip(range(1, ny), y_numbers):
        links.wait(number, y_view(mine, links.at("y", -d)))
    serve(2)
    for step in gather_tensor(lambda chip, core: gram_all.at[2 * chip + core], cut_rows):
        step()
    for b, (i, j) in enumerate(blocks):
        for s in range(nt):
            sym[NB * i + fine * s : NB * i + fine * s + fine, NB * j : NB * j + NB] = gram_all[
                s, b * fine : b * fine + fine, :
            ]

    eye = jnp.where(
        lax.broadcasted_iota(jnp.int32, (NB, NB), 0) == lax.broadcasted_iota(jnp.int32, (NB, NB), 1), 1.0, 0.0
    ).astype(f32)
    low[...] = jnp.zeros_like(low)
    inverse[...] = jnp.zeros_like(inverse)
    for k in range(nb):
        s = slice(NB * k, NB * k + NB)
        work[:, :NB] = sym[s, s]
        work[:, NB:] = eye
        for g in range(0, 16, 4):
            factor_groups(work, diag_inv, g, g + 4)
            serve(2)
        block_inv = diag_inv[...]
        inverse[s, s] = block_inv
        if k:
            inverse[s, 0 : NB * k] = exact_dot(block_inv, low[s, 0 : NB * k])
        if k < nb - 1:
            upper = exact_dot(block_inv, sym[s, NB * k + NB :])
            for i in range(k + 1, nb):
                column = upper[:, NB * (i - k - 1) : NB * (i - k)]
                sym[NB * i : NB * i + NB, NB * i :] -= exact_dot(
                    column, upper[:, NB * (i - k - 1) :], ((0,), (0,))
                )
            low[NB * k + NB :, 0 : NB * k + NB] -= exact_dot(upper, inverse[s, 0 : NB * k + NB], ((0,), (0,)))
        serve(1)
    serve(len(hooks))

    inverse_parts = split2(inverse[...])
    left_own[...] = exact_dot(share_of(full, links.x, links.c)[...], inverse[...], ((1,), (1,)))
    left_copy = pltpu.make_async_copy(left_own, left_hbm, store_sems.at[0])
    left_copy.start()
    for j in range(width // 256):
        cols = slice(256 * j, 256 * j + 256)
        block = dot3(inverse_parts, split2(wide_all[:, cols]))
        coef_t[:, cols] = ((mu_value - 1.0) * block).astype(bf16)
        for q in range(2):
            for r in range(rank // 128):
                coef[256 * j + 128 * q : 256 * j + 128 * q + 128, 128 * r : 128 * r + 128] = block[
                    128 * r : 128 * r + 128, 128 * q : 128 * q + 128
                ].T
    value = coef[...]
    mine = squares.at[links.t]
    mine[...] = jnp.broadcast_to(jnp.sum(value * value, axis=0, keepdims=True), (8, rank))
    numbers = []
    for d in range(nx):
        for core in (0, 1):
            if d or core:
                other = 2 * links.at("x", -d) + (1 - links.c if core else links.c)
                numbers.append((links.send(mine, mine, links.device(dx=d, core=core)), other))
    stores = []
    step_rows = rows // nx
    for k in range(nx):
        span = slice(k * step_rows, (k + 1) * step_rows)
        left_bf[span] = dot3(split2(full[span]), inverse_parts, ((1,), (1,))).astype(bf16)
        blend[span] = blend[span] + dot(left_bf[span], coef_t[...])
        copy = pltpu.make_async_copy(blend.at[span], out_hbm.at[span], store_sems.at[1 + k])
        copy.start()
        stores.append(copy)
    for number, other in numbers:
        links.wait(number, squares.at[other])
    total = squares[0]
    for i in range(1, nt):
        total = total + squares[i]
    scale = 1.0 / jnp.sqrt(total[0:1, :] + eps_value)
    newb[...] = (coef[...] * scale).astype(bf16)
    newb_copy = pltpu.make_async_copy(newb, newb_hbm, store_sems.at[1 + nx])
    newb_copy.start()
    for copy in links.sent:
        copy.wait_send()
    left_copy.wait()
    for copy in stores:
        copy.wait()
    newb_copy.wait()


def body(dims, momentum, gradient, basis):
    nx, ny, nz = dims
    nt = 2 * nx
    rows, width = momentum.shape
    rank = basis.shape[1]
    share = rows // nt
    half = rank // 2
    fine = NB // nt
    nb = rank // NB
    piece_rows = nb * (nb + 1) // 2 * fine
    v = pltpu.VMEM
    scratch = [
        v((rows, width), f32), v((rows, width), bf16), v((width, rank), bf16),
        v((rows, width), bf16), v((rows, width), bf16),
        v((rows, rank), f32), v((rows // 2, rank), f32),
        v((nx // 2, share, rank), f32), v((nx // 2, share, rank), f32),
        v((rows, rank), f32),
        v((rank, rows), f32), v((rank, rows), bf16), v((rank, rows), bf16),
        v((piece_rows, NB), f32), v((ny - 1, piece_rows // ny, NB), f32), v((nz, piece_rows // ny, NB), f32),
        v((8, 128), f32), v((nt, piece_rows, NB), f32),
        v((rank, rank), f32), v((rank, rank), f32), v((NB, 2 * NB), f32), v((NB, NB), f32), v((rank, rank), f32),
        v((rank, width), f32),
        v((ny // 2, half // ny, width), f32), v((ny // 2, half // ny, width), f32),
        v((nz // 2, half // ny // nz, width), f32), v((nz // 2, half // ny // nz, width), f32),
        v((nz // 2, half // nz, width), f32), v((nz // 2, half // nz, width), f32),
        v((ny // 2, half // ny // nz, width), f32), v((ny // 2, half // ny // nz, width), f32),
        v((rank, width), f32),
        v((rank, width), bf16), v((width, rank), f32), v((nt, 8, rank), f32),
        v((rows, rank), bf16), v((share, rank), f32), v((width, rank), bf16),
        pltpu.SemaphoreType.DMA((2 * nx + 1,)), pltpu.SemaphoreType.DMA((nx + 2,)),
        pltpu.SemaphoreType.DMA((128,)), pltpu.SemaphoreType.DMA((128,)),
    ]
    hbm = pl.BlockSpec(memory_space=pl.ANY)
    return pl.pallas_call(
        functools.partial(kernel, dims),
        out_shape=(
            jax.ShapeDtypeStruct((rows, width), f32),
            jax.ShapeDtypeStruct((share, rank), f32),
            jax.ShapeDtypeStruct((width, rank), bf16),
        ),
        in_specs=[hbm, hbm, hbm],
        out_specs=(hbm, hbm, hbm),
        scratch_shapes=scratch,
        compiler_params=pltpu.CompilerParams(
            collective_id=0, has_side_effects=True, vmem_limit_bytes=56 * 2**20
        ),
    )(momentum, gradient, basis)


def solution(mesh):
    dims = (4, 4, 8)
    placed = (P("fsdp", "tensor"), P("fsdp", "tensor"), P("tensor", None))
    return jax.shard_map(
        functools.partial(body, dims),
        mesh=mesh,
        in_specs=placed,
        out_specs=(P("fsdp", "tensor"), P(("fsdp", "tensor"), None), P("tensor", None)),
        check_vma=False,
    )
```

```python
import functools

import jax
import jax.numpy as jnp
from jax import lax
from jax.experimental import pallas as pl
from jax.experimental.pallas import tpu as pltpu
from jax.sharding import PartitionSpec as P

mu_value = 0.95
eps_value = 1e-06
f32 = jnp.float32
bf16 = jnp.bfloat16
MESH = pl.DeviceIdType.MESH
HIGHEST = lax.Precision.HIGHEST
NB = 128

RING_CHUNKS = (1, 2)
PLAN = (
    "p0", "p1", "p2", "p3", "p0", "p1", "p2", "p3", "p0", "p0", "p1", "w0", "p1", "p2", "w1", "p2",
    "p3", "w2", "p3", "g", "w3", "w0", "w1", "w2", "g", "w0", "w3", "w1", "g", "w2", "w0", "w3",
    "g", "w1", "g", "f", "f", "w2", "f", "f", "w0", "f", "w3", "f", "f", "f", "f", "w1", "f", "f",
    "f", "f", "f", "w2", "f", "f", "f", "f", "f", "f", "w3", "f", "f", "f", "f", "w1", "f", "f",
    "f", "f", "w2", "f", "f", "f", "f", "w1", "f", "f", "f", "f", "w2", "l",
)


def dot(left, right, dims=((1,), (0,)), precision=None):
    return lax.dot_general(left, right, (dims, ((), ())), precision=precision, preferred_element_type=f32)


def exact_dot(left, right, dims=((1,), (0,))):
    return dot(left, right, dims, HIGHEST)


def split2(value):
    high = value.astype(bf16)
    return high, (value - high.astype(f32)).astype(bf16)


def dot3(left, right, dims=((1,), (0,))):
    left_high, left_low = left
    right_high, right_low = right
    return dot(left_high, right_high, dims) + (dot(left_low, right_high, dims) + dot(left_high, right_low, dims))


def factor_groups(work, inverse, first, last):
    for group in range(first, last):
        r0 = 8 * group
        n = NB - r0
        cols = [jnp.broadcast_to(work[r0:NB, r0 + j : r0 + j + 1], (n, 128)) for j in range(8)]
        top = work[r0 : r0 + 8, :]
        rows = []
        for k in range(8):
            inv = lax.rsqrt(cols[k][k : k + 1, :])
            c = cols[k] * inv
            cols[k] = c
            for j in range(k + 1, 8):
                cols[j] = cols[j] - c * c[j : j + 1, :]
            row = top[k : k + 1, :] * jnp.concatenate([inv, inv], axis=1)
            rows.append(row)
            if k < 7:
                top = top - jnp.concatenate([c[0:8], c[0:8]], axis=1) * row
            inverse[r0 + k : r0 + k + 1, :] = row[:, 128:]
        if n > 8:
            for half in (slice(0, 128), slice(128, 256)):
                rest = work[r0 + 8 : NB, half]
                for k in range(8):
                    rest = rest - cols[k][8:] * rows[k][:, half]
                work[r0 + 8 : NB, half] = rest


class Links:
    def __init__(self, dims, send_sems, recv_sems):
        self.nx, self.ny, self.nz = dims
        f, t = lax.axis_index("fsdp"), lax.axis_index("tensor")
        self.y, self.z = f // self.nz, lax.rem(f, self.nz)
        self.x, self.c = t // 2, lax.rem(t, 2)
        self.t, self.f = t, f
        self.send_sems, self.recv_sems = send_sems, recv_sems
        self.count = 0
        self.sent = []

    def size(self, axis):
        return {"x": self.nx, "y": self.ny, "z": self.nz}[axis]

    def pos(self, axis):
        return {"x": self.x, "y": self.y, "z": self.z}[axis]

    def at(self, axis, offset):
        n = self.size(axis)
        return lax.rem(self.pos(axis) + (offset % n), n)

    def device(self, dx=0, dy=0, dz=0, core=0):
        x, y, z = self.at("x", dx), self.at("y", dy), self.at("z", dz)
        c = 1 - self.c if core else self.c
        return (y * self.nz + z, x * 2 + c)

    def along(self, axis, offset):
        return self.device(**{"d" + axis: offset})

    def send(self, src, dst, device):
        number = self.count
        self.count += 1
        copy = pltpu.make_async_remote_copy(
            src_ref=src,
            dst_ref=dst,
            send_sem=self.send_sems.at[number],
            recv_sem=self.recv_sems.at[number],
            device_id=device,
            device_id_type=MESH,
        )
        copy.start()
        self.sent.append(copy)
        return number

    def wait(self, number, landing):
        pltpu.make_async_remote_copy(
            src_ref=landing,
            dst_ref=landing,
            send_sem=self.send_sems.at[number],
            recv_sem=self.recv_sems.at[number],
            device_id=self.device(core=1),
            device_id_type=MESH,
        ).wait_recv()


def cut(view):
    size = view.shape[0]
    return view.at[0 : size // 2], view.at[size // 2 : size]


def reduce_ring(links, axis, block, plus, minus):
    half = links.size(axis) // 2
    state = {}

    def add(target, slot, number):
        links.wait(number, slot)
        target[...] = target[...] + slot[...]

    def step(s):
        k = half + 1 - s
        ahead, behind = block(links.at(axis, k)), block(links.at(axis, -k))
        if s > 1:
            target, slot = (cut(ahead)[0], cut(plus.at[s - 2])[0]) if s == 2 else (ahead, plus.at[s - 2])
            add(target, slot, state["plus"])
        src, dst = (cut(ahead)[0], cut(plus.at[s - 1])[0]) if s == 1 else (ahead, plus.at[s - 1])
        state["plus"] = links.send(src, dst, links.along(axis, 1))
        if s > 1:
            target, slot = (cut(behind)[1], cut(minus.at[s - 2])[1]) if s == 2 else (behind, minus.at[s - 2])
            add(target, slot, state["minus"])
        src, dst = (cut(behind)[1], cut(minus.at[s - 1])[1]) if s == 1 else (behind, minus.at[s - 1])
        state["minus"] = links.send(src, dst, links.along(axis, -1))

    def last():
        own = block(links.pos(axis))
        target, slot = (cut(own)[0], cut(plus.at[0])[0]) if half == 1 else (own, plus.at[half - 1])
        add(target, slot, state["plus"])
        target, slot = (cut(own)[1], cut(minus.at[0])[1]) if half == 1 else (own, minus.at[half - 1])
        add(target, slot, state["minus"])

    return [functools.partial(step, s) for s in range(1, half + 1)] + [last]


def gather_ring(links, axis, block, on_block=None):
    n = links.size(axis)
    half = n // 2
    state = {}

    def step(s):
        ahead, behind = block(links.at(axis, 1 - s)), block(links.at(axis, s - 1))
        if s > 1:
            links.wait(state["plus"], ahead)
        view = cut(ahead)[0] if s == half else ahead
        state["plus"] = links.send(view, view, links.along(axis, 1))
        if s > 1:
            links.wait(state["minus"], behind)
        view = cut(behind)[1] if s == half else behind
        state["minus"] = links.send(view, view, links.along(axis, -1))
        if on_block is not None:
            on_block(links.at(axis, 1 - s))
            if s > 1:
                on_block(links.at(axis, s - 1))

    def last():
        far = cut(block(links.at(axis, half)))
        links.wait(state["plus"], far[0])
        links.wait(state["minus"], far[1])
        if on_block is not None:
            on_block(links.at(axis, half))

    return [functools.partial(step, s) for s in range(1, half + 1)] + [last]


def scatter_direct(links, axis, block, slots):
    n = links.size(axis)
    numbers = []

    def send():
        for d in range(1, n):
            numbers.append(links.send(block(links.at(axis, d)), slots.at[d - 1], links.along(axis, d)))

    def add():
        own = block(links.pos(axis))
        total = own[...]
        for d, number in zip(range(1, n), numbers):
            links.wait(number, slots.at[d - 1])
            total = total + slots[d - 1]
        own[...] = total

    return send, add


def gather_direct(links, axis, block, on_block=None):
    n = links.size(axis)
    numbers = []

    def send():
        own = block(links.pos(axis))
        for d in range(1, n):
            numbers.append(links.send(own, own, links.along(axis, d)))
        if on_block is not None:
            on_block(links.pos(axis))

    def wait():
        for d, number in zip(range(1, n), numbers):
            links.wait(number, block(links.at(axis, -d)))
            if on_block is not None:
                on_block(links.at(axis, -d))

    return send, wait


def chain(*steps):
    def run():
        for step in steps:
            step()

    return run


def kernel(
    dims,
    mom_hbm, grad_hbm, basis_hbm,
    out_hbm, left_hbm, newb_hbm,
    blend, grad, basis, blend_hi, blend_lo, part, from_core, x_slots,
    full, flip, flip_hi, flip_lo,
    piece, from_y, from_z, tiles, gram_all, sym, low, work, diag_inv, inverse,
    wide, y_slots, y_plus, y_minus, z_slots, wide_all,
    coef_t, coef, squares, left_bf, left_own, newb,
    load_sems, store_sems, send_sems, recv_sems,
):
    nx, ny, nz = dims
    nt = 2 * nx
    rows, width = blend.shape
    rank = basis.shape[1]
    chunk = rank // 4
    share = rows // nt
    links = Links(dims, send_sems, recv_sems)
    chip_rows = 2 * share

    loads = []
    basis_copy = pltpu.make_async_copy(basis_hbm, basis, load_sems.at[2 * nx])
    basis_copy.start()
    for k in range(nx):
        chip = links.at("x", [nx // 2, 1, nx - 1, 0][k] if nx == 4 else k + 1)
        span = pl.ds(pl.multiple_of(chip * chip_rows, chip_rows), chip_rows)
        m = pltpu.make_async_copy(mom_hbm.at[span], blend.at[span], load_sems.at[2 * k])
        g = pltpu.make_async_copy(grad_hbm.at[span], grad.at[span], load_sems.at[2 * k + 1])
        m.start()
        g.start()
        loads.append((m, g, span, chip))

    barrier = pltpu.get_barrier_semaphore()
    peers = [links.device(core=1)]
    peers += [links.device(dx=d, core=c) for d in range(1, nx) for c in (0, 1)]
    peers += [links.along("y", d) for d in range(1, ny)]
    peers += [links.along("z", d) for d in range(1, nz)]
    peers += [links.device(dx=dx, dy=dy) for dx in range(1, nx) for dy in range(1, ny)]
    for peer in peers:
        pl.semaphore_signal(barrier, inc=1, device_id=peer, device_id_type=MESH)

    def share_of(ref, chip, core):
        return ref.at[:, pl.ds(pl.multiple_of((2 * chip + core) * share, share), share)]

    def joined(*pieces):
        return jnp.concatenate(pieces, axis=1)

    basis_copy.wait()
    core_numbers = []
    for m, g, span, chip in loads:
        m.wait()
        g.wait()
        value = blend[span] + grad[span].astype(f32)
        blend[span] = value
        high = value.astype(bf16)
        rest = value - high.astype(f32)
        mid = rest.astype(bf16)
        tail = (rest - mid.astype(f32)).astype(bf16)
        blend_hi[span] = high
        blend_lo[span] = mid
        q = basis[...]
        product = dot(high, q) + (dot(mid, q) + dot(tail, q))
        for j in range(4):
            part[j, span, :] = product[:, j * chunk : (j + 1) * chunk]
        if not core_numbers:
            pl.semaphore_wait(barrier, len(peers))
        number = links.send(
            share_of(part, chip, 1 - links.c), from_core.at[:, pl.ds(chip * share, share)], links.device(core=1)
        )
        core_numbers.append((number, chip))
    for number, chip in core_numbers:
        landing = from_core.at[:, pl.ds(chip * share, share)]
        links.wait(number, landing)
        mine = share_of(part, chip, links.c)
        mine[...] = mine[...] + landing[...]

    nb = rank // NB
    fine = NB // nt

    cols = width // nz

    def rows_of(ref, row, size):
        return ref.at[:, pl.ds(pl.multiple_of(row, 8), size)]

    def tile_of(ref, row, size, i):
        return ref.at[i, pl.ds(pl.multiple_of(row, 8), size)]

    def gather_core(view):
        numbers = []

        def to_core(chip):
            numbers.append((links.send(view(chip, links.c), view(chip, links.c), links.device(core=1)), chip))

        def finish():
            for number, chip in numbers:
                links.wait(number, view(chip, 1 - links.c))

        return to_core, finish

    def project_steps(j):
        cols = slice(j * chunk, (j + 1) * chunk)

        def partial_view(chip):
            return share_of(part, chip, links.c).at[j]

        def full_view(chip, core):
            return share_of(full, chip, core).at[j]

        def keep():
            full_view(links.x, links.c)[...] = partial_view(links.x)[...]

        def turn():
            for i in range(rows // 128):
                block = full[j, 128 * i : 128 * i + 128, :].T
                flip[cols, 128 * i : 128 * i + 128] = block
                high, lower = split2(block)
                flip_hi[cols, 128 * i : 128 * i + 128] = high
                flip_lo[cols, 128 * i : 128 * i + 128] = lower

        send, add = scatter_direct(links, "x", partial_view, x_slots.at[j])
        to_core, finish = gather_core(full_view)
        share_out, wait = gather_direct(links, "x", lambda i: full_view(i, links.c), to_core)
        return [send, chain(add, keep, share_out), wait, chain(finish, turn)]

    def wide_steps(j, ring):
        base, size = j * chunk, chunk // ny
        mine = base + links.y * size
        span = slice(base, base + chunk)

        def multiply():
            for n in range(width // 256):
                part_cols = slice(256 * n, 256 * n + 256)
                values = dot3((flip_hi[span, :], flip_lo[span, :]), (blend_hi[:, part_cols], blend_lo[:, part_cols]))
                for m in range(256 // cols):
                    wide[256 // cols * n + m, span, :] = values[:, cols * m : cols * m + cols]

        def keep():
            tile_of(wide_all, mine, size, links.z)[...] = tile_of(wide, mine, size, links.z)[...]

        z_send, z_add = scatter_direct(links, "z", functools.partial(tile_of, wide, mine, size), z_slots.at[j])
        z_share, z_wait = gather_direct(links, "z", functools.partial(tile_of, wide_all, mine, size))
        middle = chain(z_add, keep, z_share)

        def y_block(ref, i):
            return rows_of(ref, base + i * size, size)

        if ring:
            out = reduce_ring(links, "y", functools.partial(y_block, wide), y_plus.at[j], y_minus.at[j])
            back = gather_ring(links, "y", functools.partial(y_block, wide_all))
            return (
                [chain(multiply, out[0])] + out[1:-1] + [chain(out[-1], z_send), middle, chain(z_wait, back[0])]
                + back[1:]
            )
        y_send, y_add = scatter_direct(links, "y", functools.partial(y_block, wide), y_slots.at[j])
        y_share, y_wait = gather_direct(links, "y", functools.partial(y_block, wide_all))
        return [chain(multiply, y_send), chain(y_add, z_send), middle, chain(z_wait, y_share), y_wait]

    blocks = [(i, j) for i in range(nb) for j in range(i, nb)]
    y_rows = len(blocks) * fine // ny

    def gram_y(ref, i):
        return ref.at[pl.ds(pl.multiple_of(i * y_rows, 8), y_rows)]

    def gram_steps():
        gy_send, gy_add = scatter_direct(links, "y", functools.partial(gram_y, piece), from_y)
        gz_send, gz_wait = gather_direct(links, "z", lambda i: from_z.at[i])
        to_core, finish = gather_core(lambda chip, core: gram_all.at[2 * chip + core])
        numbers = {}

        def strip():
            picked = jnp.concatenate(
                [flip[pl.ds(pl.multiple_of(NB * i + fine * links.t, 8), fine), :] for i in range(nb)], axis=0
            )
            values = joined(*[exact_dot(picked, joined(full[j], full[j + 1])) for j in (0, 2)])
            for b, (i, j) in enumerate(blocks):
                piece[b * fine : b * fine + fine, :] = values[i * fine : i * fine + fine, NB * j : NB * j + NB]
            gy_send()

        def along_z():
            gy_add()
            from_z[links.z] = gram_y(piece, links.y)[...]
            gz_send()

        def along_xy():
            gz_wait()
            total = from_z[0]
            for i in range(1, nz):
                total = total + from_z[i]
            mine = gram_y(gram_all.at[links.t], links.y)
            mine[...] = total
            for dx in range(nx):
                for dy in range(ny):
                    if dx or dy:
                        numbers[dx, dy] = links.send(mine, mine, links.device(dx=dx, dy=dy))

        def wait_xy():
            for dx in range(nx):
                chip = links.at("x", -dx)
                for dy in range(ny):
                    if dx or dy:
                        links.wait(numbers[dx, dy], gram_y(gram_all.at[2 * chip + links.c], links.at("y", -dy)))
                to_core(chip)

        def assemble():
            finish()
            for b, (i, j) in enumerate(blocks):
                for s in range(nt):
                    sym[NB * i + fine * s : NB * i + fine * s + fine, NB * j : NB * j + NB] = gram_all[
                        s, b * fine : b * fine + fine, :
                    ]

        return [strip, along_z, along_xy, wait_xy, assemble]

    def factor():
        eye = jnp.where(
            lax.broadcasted_iota(jnp.int32, (NB, NB), 0) == lax.broadcasted_iota(jnp.int32, (NB, NB), 1), 1.0, 0.0
        ).astype(f32)
        low[...] = jnp.zeros_like(low)
        inverse[...] = jnp.zeros_like(inverse)
        for k in range(nb):
            s = slice(NB * k, NB * k + NB)
            work[:, :NB] = sym[s, s]
            work[:, NB:] = eye
            for g in range(0, 16, 2):
                factor_groups(work, diag_inv, g, g + 2)
                yield
            block_inv = diag_inv[...]
            inverse[s, s] = block_inv
            if k:
                inverse[s, 0 : NB * k] = exact_dot(block_inv, low[s, 0 : NB * k])
            if k < nb - 1:
                upper = exact_dot(block_inv, sym[s, NB * k + NB :])
                for i in range(k + 1, nb):
                    column = upper[:, NB * (i - k - 1) : NB * (i - k)]
                    sym[NB * i : NB * i + NB, NB * i :] -= exact_dot(
                        column, upper[:, NB * (i - k - 1) :], ((0,), (0,))
                    )
                low[NB * k + NB :, 0 : NB * k + NB] -= exact_dot(upper, inverse[s, 0 : NB * k + NB], ((0,), (0,)))
            yield

    stores = []

    def left():
        inverse_parts = split2(inverse[...])
        mine = share_of(full, links.x, links.c)
        left_own[...] = exact_dot(joined(*[mine[j] for j in range(4)]), inverse[...], ((1,), (1,)))
        copy = pltpu.make_async_copy(left_own, left_hbm, store_sems.at[0])
        copy.start()
        stores.append(copy)
        for k in range(nx):
            span = slice(k * chip_rows, (k + 1) * chip_rows)
            values = split2(joined(*[full[j, span, :] for j in range(4)]))
            left_bf[span] = dot3(values, inverse_parts, ((1,), (1,))).astype(bf16)

    work_lists = {"g": gram_steps(), "l": [left], "f": factor()}
    for j in range(4):
        work_lists["p%d" % j] = project_steps(j)
        work_lists["w%d" % j] = wide_steps(j, j in RING_CHUNKS)
    for name in PLAN:
        if name == "f":
            next(work_lists["f"])
        else:
            work_lists[name].pop(0)()
    assert not any(work_lists[name] for name in work_lists if name != "f")
    assert next(work_lists["f"], None) is None
    inverse_parts = split2(inverse[...])
    lanes = cols
    for j in range(width // 256):
        cols = slice(256 * j, 256 * j + 256)
        block = dot3(inverse_parts, split2(joined(*[wide_all[256 // lanes * j + m] for m in range(256 // lanes)])))
        coef_t[:, cols] = ((mu_value - 1.0) * block).astype(bf16)
        for q in range(2):
            for r in range(rank // 128):
                coef[256 * j + 128 * q : 256 * j + 128 * q + 128, 128 * r : 128 * r + 128] = block[
                    128 * r : 128 * r + 128, 128 * q : 128 * q + 128
                ].T
    value = coef[...]
    mine = squares.at[links.t]
    mine[...] = jnp.broadcast_to(jnp.sum(value * value, axis=0, keepdims=True), (8, rank))
    numbers = []
    for d in range(nx):
        for core in (0, 1):
            if d or core:
                other = 2 * links.at("x", -d) + (1 - links.c if core else links.c)
                numbers.append((links.send(mine, mine, links.device(dx=d, core=core)), other))
    for k in range(nx):
        span = slice(k * chip_rows, (k + 1) * chip_rows)
        blend[span] = blend[span] + dot(left_bf[span], coef_t[...])
        copy = pltpu.make_async_copy(blend.at[span], out_hbm.at[span], store_sems.at[1 + k])
        copy.start()
        stores.append(copy)
    for number, other in numbers:
        links.wait(number, squares.at[other])
    total = squares[0]
    for i in range(1, nt):
        total = total + squares[i]
    scale = 1.0 / jnp.sqrt(total[0:1, :] + eps_value)
    newb[...] = (coef[...] * scale).astype(bf16)
    newb_copy = pltpu.make_async_copy(newb, newb_hbm, store_sems.at[1 + nx])
    newb_copy.start()
    for copy in links.sent:
        copy.wait_send()
    for copy in stores:
        copy.wait()
    newb_copy.wait()


def body(dims, momentum, gradient, basis):
    nx, ny, nz = dims
    nt = 2 * nx
    rows, width = momentum.shape
    rank = basis.shape[1]
    share = rows // nt
    chunk = rank // 4
    fine = NB // nt
    nb = rank // NB
    piece_rows = nb * (nb + 1) // 2 * fine
    v = pltpu.VMEM
    scratch = [
        v((rows, width), f32), v((rows, width), bf16), v((width, rank), bf16),
        v((rows, width), bf16), v((rows, width), bf16),
        v((4, rows, chunk), f32), v((4, rows // 2, chunk), f32),
        v((4, nx - 1, share, rank // 4), f32),
        v((4, rows, chunk), f32),
        v((rank, rows), f32), v((rank, rows), bf16), v((rank, rows), bf16),
        v((piece_rows, NB), f32), v((ny - 1, piece_rows // ny, NB), f32), v((nz, piece_rows // ny, NB), f32),
        v((8, 128), f32), v((nt, piece_rows, NB), f32),
        v((rank, rank), f32), v((rank, rank), f32), v((NB, 2 * NB), f32), v((NB, NB), f32), v((rank, rank), f32),
        v((nz, rank, width // nz), f32),
        v((4, ny - 1, nz, chunk // ny, width // nz), f32),
        v((4, ny // 2, nz, chunk // ny, width // nz), f32), v((4, ny // 2, nz, chunk // ny, width // nz), f32),
        v((4, nz - 1, chunk // ny, width // nz), f32),
        v((nz, rank, width // nz), f32),
        v((rank, width), bf16), v((width, rank), f32), v((nt, 8, rank), f32),
        v((rows, rank), bf16), v((share, rank), f32), v((width, rank), bf16),
        pltpu.SemaphoreType.DMA((2 * nx + 1,)), pltpu.SemaphoreType.DMA((nx + 2,)),
        pltpu.SemaphoreType.DMA((192,)), pltpu.SemaphoreType.DMA((192,)),
    ]
    hbm = pl.BlockSpec(memory_space=pl.ANY)
    results = pl.pallas_call(
        functools.partial(kernel, dims),
        out_shape=(
            jax.ShapeDtypeStruct((rows, width), f32),
            jax.ShapeDtypeStruct((share, rank), f32),
            jax.ShapeDtypeStruct((width, rank), bf16),
        ),
        in_specs=[hbm, hbm, hbm],
        out_specs=(hbm, hbm, hbm),
        scratch_shapes=scratch,
        compiler_params=pltpu.CompilerParams(
            collective_id=0, has_side_effects=True, vmem_limit_bytes=58 * 2**20
        ),
    )(momentum, gradient, basis)
    return pl.pallas_call(
        hand_over,
        out_shape=tuple(jax.ShapeDtypeStruct(r.shape, r.dtype) for r in results),
        in_specs=[hbm, hbm, hbm],
        out_specs=(hbm, hbm, hbm),
        scratch_shapes=[pltpu.VMEM(r.shape, r.dtype) for r in results] + [pltpu.SemaphoreType.DMA((20,))],
        compiler_params=pltpu.CompilerParams(vmem_limit_bytes=32 * 2**20),
    )(*results)


def hand_over(big, left, newb, big_out, left_out, newb_out, big_v, left_v, newb_v, sems):
    size = big.shape[0] // 8
    parts = [(big.at[pl.ds(size * i, size)], big_v.at[pl.ds(size * i, size)], big_out.at[pl.ds(size * i, size)])
             for i in range(8)]
    parts += [(left, left_v, left_out), (newb, newb_v, newb_out)]
    reads = [pltpu.make_async_copy(src, mid, sems.at[i]) for i, (src, mid, _) in enumerate(parts)]
    writes = [pltpu.make_async_copy(mid, dst, sems.at[10 + i]) for i, (_, mid, dst) in enumerate(parts)]
    for copy in reads:
        copy.start()
    for read, write in zip(reads, writes):
        read.wait()
        write.start()
    for write in writes:
        write.wait()


def solution(mesh):
    dims = (4, 4, 8)
    placed = (P("fsdp", "tensor"), P("fsdp", "tensor"), P("tensor", None))
    return jax.shard_map(
        functools.partial(body, dims),
        mesh=mesh,
        in_specs=placed,
        out_specs=(P("fsdp", "tensor"), P(("fsdp", "tensor"), None), P("tensor", None)),
        check_vma=False,
    )
```

```python
import functools

import jax
import jax.numpy as jnp
from jax import lax
from jax.experimental import pallas as pl
from jax.experimental.pallas import tpu as pltpu
from jax.sharding import PartitionSpec as P

mu_value = 0.95
eps_value = 1e-06
f32 = jnp.float32
bf16 = jnp.bfloat16
MESH = pl.DeviceIdType.MESH
HIGHEST = lax.Precision.HIGHEST
NB = 128

KINDS = ('C', 'A1', 'C', 'C')
PLAN = (
    "p0", "p1", "p2", "p3", "p0", "p1", "p2", "p3", "p0", "p0", "p1", "w0", "p1", "ga", "p2", "w1",
    "p3", "p2", "w2", "p3", "gb", "ga", "w0", "w3", "w2", "w1", "gb", "ga", "w3", "w0", "w2", "ga",
    "w1", "ga", "w3", "gb", "f", "f", "w0", "f", "f", "w2", "f", "f", "f", "f", "w1", "f", "w3",
    "f", "gb", "f", "w0", "f", "f", "gb", "w2", "f", "f", "f", "f", "f", "w3", "f", "w1", "f", "f",
    "f", "w0", "f", "f", "f", "f", "w2", "f", "f", "f", "f", "w3", "f", "f", "w0", "f", "f", "f",
    "f", "w2", "l", "w3",
)


def dot(left, right, dims=((1,), (0,)), precision=None):
    return lax.dot_general(left, right, (dims, ((), ())), precision=precision, preferred_element_type=f32)


def exact_dot(left, right, dims=((1,), (0,))):
    return dot(left, right, dims, HIGHEST)


def split2(value):
    high = value.astype(bf16)
    return high, (value - high.astype(f32)).astype(bf16)


def dot3(left, right, dims=((1,), (0,))):
    left_high, left_low = left
    right_high, right_low = right
    return dot(left_high, right_high, dims) + (dot(left_low, right_high, dims) + dot(left_high, right_low, dims))


def factor_groups(work, inverse, first, last):
    for group in range(first, last):
        r0 = 8 * group
        n = NB - r0
        cols = [jnp.broadcast_to(work[r0:NB, r0 + j : r0 + j + 1], (n, 128)) for j in range(8)]
        top = work[r0 : r0 + 8, :]
        rows = []
        for k in range(8):
            inv = lax.rsqrt(cols[k][k : k + 1, :])
            c = cols[k] * inv
            cols[k] = c
            for j in range(k + 1, 8):
                cols[j] = cols[j] - c * c[j : j + 1, :]
            row = top[k : k + 1, :] * jnp.concatenate([inv, inv], axis=1)
            rows.append(row)
            if k < 7:
                top = top - jnp.concatenate([c[0:8], c[0:8]], axis=1) * row
            inverse[r0 + k : r0 + k + 1, :] = row[:, 128:]
        if n > 8:
            for half in (slice(0, 128), slice(128, 256)):
                rest = work[r0 + 8 : NB, half]
                for k in range(8):
                    rest = rest - cols[k][8:] * rows[k][:, half]
                work[r0 + 8 : NB, half] = rest


class Links:
    def __init__(self, dims, send_sems, recv_sems):
        self.nx, self.ny, self.nz = dims
        f, t = lax.axis_index("fsdp"), lax.axis_index("tensor")
        self.y, self.z = f // self.nz, lax.rem(f, self.nz)
        self.x, self.c = t // 2, lax.rem(t, 2)
        self.t, self.f = t, f
        self.send_sems, self.recv_sems = send_sems, recv_sems
        self.count = 0
        self.sent = []

    def size(self, axis):
        return {"x": self.nx, "y": self.ny, "z": self.nz}[axis]

    def pos(self, axis):
        return {"x": self.x, "y": self.y, "z": self.z}[axis]

    def at(self, axis, offset):
        n = self.size(axis)
        return lax.rem(self.pos(axis) + (offset % n), n)

    def device(self, dx=0, dy=0, dz=0, core=0):
        x, y, z = self.at("x", dx), self.at("y", dy), self.at("z", dz)
        c = 1 - self.c if core else self.c
        return (y * self.nz + z, x * 2 + c)

    def along(self, axis, offset):
        return self.device(**{"d" + axis: offset})

    def send(self, src, dst, device):
        number = self.count
        self.count += 1
        copy = pltpu.make_async_remote_copy(
            src_ref=src,
            dst_ref=dst,
            send_sem=self.send_sems.at[number],
            recv_sem=self.recv_sems.at[number],
            device_id=device,
            device_id_type=MESH,
        )
        copy.start()
        self.sent.append(copy)
        return number

    def wait(self, number, landing):
        pltpu.make_async_remote_copy(
            src_ref=landing,
            dst_ref=landing,
            send_sem=self.send_sems.at[number],
            recv_sem=self.recv_sems.at[number],
            device_id=self.device(core=1),
            device_id_type=MESH,
        ).wait_recv()


def cut(view):
    size = view.shape[0]
    return view.at[0 : size // 2], view.at[size // 2 : size]


def reduce_ring(links, axis, block, plus, minus):
    half = links.size(axis) // 2
    state = {}

    def add(target, slot, number):
        links.wait(number, slot)
        target[...] = target[...] + slot[...]

    def step(s):
        k = half + 1 - s
        ahead, behind = block(links.at(axis, k)), block(links.at(axis, -k))
        if s > 1:
            target, slot = (cut(ahead)[0], cut(plus.at[s - 2])[0]) if s == 2 else (ahead, plus.at[s - 2])
            add(target, slot, state["plus"])
        src, dst = (cut(ahead)[0], cut(plus.at[s - 1])[0]) if s == 1 else (ahead, plus.at[s - 1])
        state["plus"] = links.send(src, dst, links.along(axis, 1))
        if s > 1:
            target, slot = (cut(behind)[1], cut(minus.at[s - 2])[1]) if s == 2 else (behind, minus.at[s - 2])
            add(target, slot, state["minus"])
        src, dst = (cut(behind)[1], cut(minus.at[s - 1])[1]) if s == 1 else (behind, minus.at[s - 1])
        state["minus"] = links.send(src, dst, links.along(axis, -1))

    def last():
        own = block(links.pos(axis))
        target, slot = (cut(own)[0], cut(plus.at[0])[0]) if half == 1 else (own, plus.at[half - 1])
        add(target, slot, state["plus"])
        target, slot = (cut(own)[1], cut(minus.at[0])[1]) if half == 1 else (own, minus.at[half - 1])
        add(target, slot, state["minus"])

    return [functools.partial(step, s) for s in range(1, half + 1)] + [last]


def gather_ring(links, axis, block, on_block=None):
    n = links.size(axis)
    half = n // 2
    state = {}

    def step(s):
        ahead, behind = block(links.at(axis, 1 - s)), block(links.at(axis, s - 1))
        if s > 1:
            links.wait(state["plus"], ahead)
        view = cut(ahead)[0] if s == half else ahead
        state["plus"] = links.send(view, view, links.along(axis, 1))
        if s > 1:
            links.wait(state["minus"], behind)
        view = cut(behind)[1] if s == half else behind
        state["minus"] = links.send(view, view, links.along(axis, -1))
        if on_block is not None:
            on_block(links.at(axis, 1 - s))
            if s > 1:
                on_block(links.at(axis, s - 1))

    def last():
        far = cut(block(links.at(axis, half)))
        links.wait(state["plus"], far[0])
        links.wait(state["minus"], far[1])
        if on_block is not None:
            on_block(links.at(axis, half))

    return [functools.partial(step, s) for s in range(1, half + 1)] + [last]


def scatter_direct(links, axis, block, slots, stride=1):
    offsets = range(stride, links.size(axis), stride)
    numbers = []

    def send():
        for i, d in enumerate(offsets):
            numbers.append(links.send(block(links.at(axis, d)), slots.at[i], links.along(axis, d)))

    def add():
        own = block(links.pos(axis))
        total = own[...]
        for i, number in enumerate(numbers):
            links.wait(number, slots.at[i])
            total = total + slots[i]
        own[...] = total

    return send, add


def gather_direct(links, axis, block, on_block=None, stride=1):
    offsets = range(stride, links.size(axis), stride)
    numbers = []

    def send():
        own = block(links.pos(axis))
        for d in offsets:
            numbers.append(links.send(own, own, links.along(axis, d)))
        if on_block is not None:
            on_block(links.pos(axis))

    def wait():
        for d, number in zip(offsets, numbers):
            links.wait(number, block(links.at(axis, -d)))
            if on_block is not None:
                on_block(links.at(axis, -d))

    return send, wait


def chain(*steps):
    def run():
        for step in steps:
            step()

    return run


def kernel(
    dims,
    mom_hbm, grad_hbm, basis_hbm,
    out_hbm, left_hbm, newb_hbm,
    blend, grad, basis, blend_hi, blend_lo, part, from_core, x_slots,
    full, flip, flip_hi, flip_lo,
    piece_a, from_y_a, from_z_a, gram_a, piece_b, from_y_b, from_z_b, gram_b, sym, low, work, diag_inv, inverse,
    wide, y_slots, y_plus, y_minus, z_slots, pair_slots, wide_all,
    coef_t, coef, squares, left_bf, left_own, newb,
    load_sems, store_sems, send_sems, recv_sems,
):
    nx, ny, nz = dims
    nt = 2 * nx
    rows, width = blend.shape
    rank = basis.shape[1]
    chunk = rank // 4
    share = rows // nt
    links = Links(dims, send_sems, recv_sems)
    chip_rows = 2 * share

    loads = []
    basis_copy = pltpu.make_async_copy(basis_hbm, basis, load_sems.at[2 * nx])
    basis_copy.start()
    for k in range(nx):
        chip = links.at("x", [nx // 2, 1, nx - 1, 0][k] if nx == 4 else k + 1)
        span = pl.ds(pl.multiple_of(chip * chip_rows, chip_rows), chip_rows)
        m = pltpu.make_async_copy(mom_hbm.at[span], blend.at[span], load_sems.at[2 * k])
        g = pltpu.make_async_copy(grad_hbm.at[span], grad.at[span], load_sems.at[2 * k + 1])
        m.start()
        g.start()
        loads.append((m, g, span, chip))

    barrier = pltpu.get_barrier_semaphore()
    peers = [links.device(core=1)]
    peers += [links.device(dx=d, core=c) for d in range(1, nx) for c in (0, 1)]
    peers += [links.along("y", d) for d in range(1, ny)]
    peers += [links.along("z", d) for d in range(1, nz)]
    peers += [links.device(dx=dx, dy=dy) for dx in range(1, nx) for dy in range(1, ny)]
    for peer in peers:
        pl.semaphore_signal(barrier, inc=1, device_id=peer, device_id_type=MESH)

    def share_of(ref, chip, core):
        return ref.at[:, pl.ds(pl.multiple_of((2 * chip + core) * share, share), share)]

    def joined(*pieces):
        return jnp.concatenate(pieces, axis=1)

    basis_copy.wait()
    core_numbers = []
    for m, g, span, chip in loads:
        m.wait()
        g.wait()
        value = blend[span] + grad[span].astype(f32)
        blend[span] = value
        high = value.astype(bf16)
        rest = value - high.astype(f32)
        mid = rest.astype(bf16)
        tail = (rest - mid.astype(f32)).astype(bf16)
        blend_hi[span] = high
        blend_lo[span] = mid
        q = basis[...]
        product = dot(high, q) + (dot(mid, q) + dot(tail, q))
        for j in range(4):
            part[j, span, :] = product[:, j * chunk : (j + 1) * chunk]
        if not core_numbers:
            pl.semaphore_wait(barrier, len(peers))
        number = links.send(
            share_of(part, chip, 1 - links.c), from_core.at[:, pl.ds(chip * share, share)], links.device(core=1)
        )
        core_numbers.append((number, chip))
    for number, chip in core_numbers:
        landing = from_core.at[:, pl.ds(chip * share, share)]
        links.wait(number, landing)
        mine = share_of(part, chip, links.c)
        mine[...] = mine[...] + landing[...]

    nb = rank // NB
    fine = NB // nt

    cols = width // nz

    def rows_of(ref, row, size):
        return ref.at[:, :, pl.ds(pl.multiple_of(row, 8), size)]

    def tile_of(ref, row, size, i):
        return ref.at[lax.rem(i, 2), i // 2, pl.ds(pl.multiple_of(row, 8), size)]

    parity = lax.rem(links.z, 2)
    turn_z = 1 - 2 * parity
    pair_devices = [
        (links.y * nz + lax.rem(links.z + nz + sign * turn_z, nz), links.t) for sign in (1, -1)
    ]

    def gather_core(view):
        numbers = []

        def to_core(chip):
            numbers.append((links.send(view(chip, links.c), view(chip, links.c), links.device(core=1)), chip))

        def finish():
            for number, chip in numbers:
                links.wait(number, view(chip, 1 - links.c))

        return to_core, finish

    def project_steps(j):
        cols = slice(j * chunk, (j + 1) * chunk)

        def partial_view(chip):
            return share_of(part, chip, links.c).at[j]

        def full_view(chip, core):
            return share_of(full, chip, core).at[j]

        def keep():
            full_view(links.x, links.c)[...] = partial_view(links.x)[...]

        def turn():
            for i in range(rows // 128):
                block = full[j, 128 * i : 128 * i + 128, :].T
                flip[cols, 128 * i : 128 * i + 128] = block
                high, lower = split2(block)
                flip_hi[cols, 128 * i : 128 * i + 128] = high
                flip_lo[cols, 128 * i : 128 * i + 128] = lower

        send, add = scatter_direct(links, "x", partial_view, x_slots.at[j])
        to_core, finish = gather_core(full_view)
        share_out, wait = gather_direct(links, "x", lambda i: full_view(i, links.c), to_core)
        return [send, chain(add, keep, share_out), wait, chain(finish, turn)]

    def wide_steps(j, kind):
        base, size = j * chunk, chunk // ny
        mine = base + links.y * size
        span = slice(base, base + chunk)

        def multiply():
            for n in range(width // 256):
                part_cols = slice(256 * n, 256 * n + 256)
                values = dot3((flip_hi[span, :], flip_lo[span, :]), (blend_hi[:, part_cols], blend_lo[:, part_cols]))
                for m in range(256 // cols):
                    tile = 256 // cols * n + m
                    wide[tile % 2, tile // 2, span, :] = values[:, cols * m : cols * m + cols]

        def keep():
            tile_of(wide_all, mine, size, links.z)[...] = tile_of(wide, mine, size, links.z)[...]

        z_send, z_add = scatter_direct(links, "z", functools.partial(tile_of, wide, mine, size), z_slots.at[j])
        z_share, z_wait = gather_direct(links, "z", functools.partial(tile_of, wide_all, mine, size))
        middle = chain(z_add, keep, z_share)

        def y_block(ref, i):
            return rows_of(ref, base + i * size, size)

        if kind == "C":
            numbers = []

            def side(ref, which, h):
                return ref.at[which, :, base + h * (chunk // 2) : base + (h + 1) * (chunk // 2)]

            def pair_send():
                for h in (0, 1):
                    numbers.append(links.send(side(wide, 1 - parity, h), pair_slots.at[j, h], pair_devices[h]))

            def pair_add():
                for h in (0, 1):
                    links.wait(numbers[h], pair_slots.at[j, h])
                    mine_side = side(wide, parity, h)
                    mine_side[...] = mine_side[...] + pair_slots[j, h]

            def pair_share():
                for h in (0, 1):
                    view = side(wide_all, parity, h)
                    numbers.append(links.send(view, view, pair_devices[h]))

            def pair_wait():
                for h in (0, 1):
                    links.wait(numbers[2 + h], side(wide_all, 1 - parity, h))

            def half_block(ref, i):
                return ref.at[parity, :, pl.ds(pl.multiple_of(base + i * size, 8), size)]

            y_send, y_add = scatter_direct(links, "y", functools.partial(half_block, wide), y_slots.at[j, :, 0])
            y_share, y_wait = gather_direct(links, "y", functools.partial(half_block, wide_all))
            z_send, z_add = scatter_direct(
                links, "z", functools.partial(tile_of, wide, mine, size), z_slots.at[j], 2
            )
            z_share, z_wait = gather_direct(links, "z", functools.partial(tile_of, wide_all, mine, size), None, 2)
            return [
                chain(multiply, pair_send), chain(pair_add, y_send), chain(y_add, z_send),
                chain(z_add, keep, z_share), chain(z_wait, y_share), chain(y_wait, pair_share), pair_wait,
            ]
        if kind == "A2":
            out = reduce_ring(links, "y", functools.partial(y_block, wide), y_plus.at[j], y_minus.at[j])
            back = gather_ring(links, "y", functools.partial(y_block, wide_all))
            return (
                [chain(multiply, out[0])] + out[1:-1] + [chain(out[-1], z_send), middle, chain(z_wait, back[0])]
                + back[1:]
            )
        y_send, y_add = scatter_direct(links, "y", functools.partial(y_block, wide), y_slots.at[j])
        y_share, y_wait = gather_direct(links, "y", functools.partial(y_block, wide_all))
        return [chain(multiply, y_send), chain(y_add, z_send), middle, chain(z_wait, y_share), y_wait]

    def gram_steps(first_col, row_blocks, piece, from_y, from_z, gathered):
        y_rows = piece.shape[0] // ny
        tiles = [(i, j) for i in range(row_blocks) for j in (first_col, first_col + 1)]

        def y_part(ref, i):
            return ref.at[pl.ds(pl.multiple_of(i * y_rows, 8), y_rows)]

        gy_send, gy_add = scatter_direct(links, "y", functools.partial(y_part, piece), from_y)
        gz_send, gz_wait = gather_direct(links, "z", lambda i: from_z.at[i])
        to_core, finish = gather_core(lambda chip, core: gathered.at[2 * chip + core])
        numbers = {}

        def strip():
            picked = jnp.concatenate(
                [flip[pl.ds(pl.multiple_of(NB * i + fine * links.t, 8), fine), :] for i in range(row_blocks)], axis=0
            )
            values = exact_dot(picked, joined(full[first_col], full[first_col + 1]))
            for b, (i, j) in enumerate(tiles):
                c = NB * (j - first_col)
                piece[b * fine : b * fine + fine, :] = values[i * fine : i * fine + fine, c : c + NB]
            gy_send()

        def along_z():
            gy_add()
            from_z[links.z] = y_part(piece, links.y)[...]
            gz_send()

        def along_xy():
            gz_wait()
            total = from_z[0]
            for i in range(1, nz):
                total = total + from_z[i]
            mine = y_part(gathered.at[links.t], links.y)
            mine[...] = total
            for dx in range(nx):
                for dy in range(ny):
                    if dx or dy:
                        numbers[dx, dy] = links.send(mine, mine, links.device(dx=dx, dy=dy))

        def wait_xy():
            for dx in range(nx):
                chip = links.at("x", -dx)
                for dy in range(ny):
                    if dx or dy:
                        links.wait(numbers[dx, dy], y_part(gathered.at[2 * chip + links.c], links.at("y", -dy)))
                to_core(chip)

        def assemble():
            finish()
            for b, (i, j) in enumerate(tiles):
                for s in range(nt):
                    sym[NB * i + fine * s : NB * i + fine * s + fine, NB * j : NB * j + NB] = gathered[
                        s, b * fine : b * fine + fine, :
                    ]

        return [strip, along_z, along_xy, wait_xy, assemble]

    def factor():
        eye = jnp.where(
            lax.broadcasted_iota(jnp.int32, (NB, NB), 0) == lax.broadcasted_iota(jnp.int32, (NB, NB), 1), 1.0, 0.0
        ).astype(f32)
        inverse[...] = jnp.zeros_like(inverse)
        low[...] = jnp.zeros_like(low)
        top, rest = slice(0, 2 * NB), slice(2 * NB, rank)
        for k in range(nb):
            s = slice(NB * k, NB * k + NB)
            if k == 2:
                upper = exact_dot(inverse[top, top], sym[top, rest])
                sym[rest, rest] -= exact_dot(upper, upper, ((0,), (0,)))
                low[rest, top] = -exact_dot(upper, inverse[top, top], ((0,), (0,)))
            work[:, :NB] = sym[s, s]
            work[:, NB:] = eye
            for g in range(0, 16, 2):
                factor_groups(work, diag_inv, g, g + 2)
                yield
            block_inv = diag_inv[...]
            inverse[s, s] = block_inv
            if k:
                inverse[s, 0 : NB * k] = exact_dot(block_inv, low[s, 0 : NB * k])
            if k % 2 == 0:
                after = slice(NB * k + NB, NB * k + 2 * NB)
                upper = exact_dot(block_inv, sym[s, after])
                sym[after, after] -= exact_dot(upper, upper, ((0,), (0,)))
                low[after, 0 : NB * k + NB] -= exact_dot(upper, inverse[s, 0 : NB * k + NB], ((0,), (0,)))
            yield

    stores = []

    def left():
        inverse_parts = split2(inverse[...])
        mine = share_of(full, links.x, links.c)
        left_own[...] = exact_dot(joined(*[mine[j] for j in range(4)]), inverse[...], ((1,), (1,)))
        copy = pltpu.make_async_copy(left_own, left_hbm, store_sems.at[0])
        copy.start()
        stores.append(copy)
        for k in range(nx):
            span = slice(k * chip_rows, (k + 1) * chip_rows)
            values = split2(joined(*[full[j, span, :] for j in range(4)]))
            left_bf[span] = dot3(values, inverse_parts, ((1,), (1,))).astype(bf16)

    work_lists = {
        "ga": gram_steps(0, nb // 2, piece_a, from_y_a, from_z_a, gram_a),
        "gb": gram_steps(nb // 2, nb, piece_b, from_y_b, from_z_b, gram_b),
        "l": [left],
        "f": factor(),
    }
    for j in range(4):
        work_lists["p%d" % j] = project_steps(j)
        work_lists["w%d" % j] = wide_steps(j, KINDS[j])
    for name in PLAN:
        if name == "f":
            next(work_lists["f"])
        else:
            work_lists[name].pop(0)()
    assert not any(work_lists[name] for name in work_lists if name != "f")
    assert next(work_lists["f"], None) is None
    inverse_parts = split2(inverse[...])
    lanes = cols
    for j in range(width // 256):
        cols = slice(256 * j, 256 * j + 256)
        block = dot3(inverse_parts, split2(joined(*[wide_all[i % 2, i // 2] for i in range(256 // lanes * j, 256 // lanes * (j + 1))])))
        coef_t[:, cols] = ((mu_value - 1.0) * block).astype(bf16)
        for q in range(2):
            for r in range(rank // 128):
                coef[256 * j + 128 * q : 256 * j + 128 * q + 128, 128 * r : 128 * r + 128] = block[
                    128 * r : 128 * r + 128, 128 * q : 128 * q + 128
                ].T
    value = coef[...]
    mine = squares.at[links.t]
    mine[...] = jnp.broadcast_to(jnp.sum(value * value, axis=0, keepdims=True), (8, rank))
    numbers = []
    for d in range(nx):
        for core in (0, 1):
            if d or core:
                other = 2 * links.at("x", -d) + (1 - links.c if core else links.c)
                numbers.append((links.send(mine, mine, links.device(dx=d, core=core)), other))
    for k in range(nx):
        span = slice(k * chip_rows, (k + 1) * chip_rows)
        blend[span] = blend[span] + dot(left_bf[span], coef_t[...])
        copy = pltpu.make_async_copy(blend.at[span], out_hbm.at[span], store_sems.at[1 + k])
        copy.start()
        stores.append(copy)
    for number, other in numbers:
        links.wait(number, squares.at[other])
    total = squares[0]
    for i in range(1, nt):
        total = total + squares[i]
    scale = 1.0 / jnp.sqrt(total[0:1, :] + eps_value)
    newb[...] = (coef[...] * scale).astype(bf16)
    newb_copy = pltpu.make_async_copy(newb, newb_hbm, store_sems.at[1 + nx])
    newb_copy.start()
    for copy in links.sent:
        copy.wait_send()
    for copy in stores:
        copy.wait()
    newb_copy.wait()


def body(dims, momentum, gradient, basis):
    nx, ny, nz = dims
    nt = 2 * nx
    rows, width = momentum.shape
    rank = basis.shape[1]
    share = rows // nt
    chunk = rank // 4
    fine = NB // nt
    v = pltpu.VMEM

    def gram_scratch(size):
        return (
            v((size, NB), f32), v((ny - 1, size // ny, NB), f32), v((nz, size // ny, NB), f32), v((nt, size, NB), f32)
        )

    scratch = [
        v((rows, width), f32), v((rows, width), bf16), v((width, rank), bf16),
        v((rows, width), bf16), v((rows, width), bf16),
        v((4, rows, chunk), f32), v((4, rows // 2, chunk), f32),
        v((4, nx - 1, share, rank // 4), f32),
        v((4, rows, chunk), f32),
        v((rank, rows), f32), v((rank, rows), bf16), v((rank, rows), bf16),
        *gram_scratch(4 * fine), *gram_scratch(8 * fine),
        v((rank, rank), f32), v((rank, rank), f32), v((NB, 2 * NB), f32), v((NB, NB), f32), v((rank, rank), f32),
        v((2, nz // 2, rank, width // nz), f32),
        v((4, ny - 1, 2, nz // 2, chunk // ny, width // nz), f32),
        v((4, ny // 2, 2, nz // 2, chunk // ny, width // nz), f32),
        v((4, ny // 2, 2, nz // 2, chunk // ny, width // nz), f32),
        v((4, nz - 1, chunk // ny, width // nz), f32), v((4, 2, nz // 2, chunk // 2, width // nz), f32),
        v((2, nz // 2, rank, width // nz), f32),
        v((rank, width), bf16), v((width, rank), f32), v((nt, 8, rank), f32),
        v((rows, rank), bf16), v((share, rank), f32), v((width, rank), bf16),
        pltpu.SemaphoreType.DMA((2 * nx + 1,)), pltpu.SemaphoreType.DMA((nx + 2,)),
        pltpu.SemaphoreType.DMA((224,)), pltpu.SemaphoreType.DMA((224,)),
    ]
    hbm = pl.BlockSpec(memory_space=pl.ANY)
    results = pl.pallas_call(
        functools.partial(kernel, dims),
        out_shape=(
            jax.ShapeDtypeStruct((rows, width), f32),
            jax.ShapeDtypeStruct((share, rank), f32),
            jax.ShapeDtypeStruct((width, rank), bf16),
        ),
        in_specs=[hbm, hbm, hbm],
        out_specs=(hbm, hbm, hbm),
        scratch_shapes=scratch,
        compiler_params=pltpu.CompilerParams(
            collective_id=0, has_side_effects=True, vmem_limit_bytes=58 * 2**20
        ),
    )(momentum, gradient, basis)
    return pl.pallas_call(
        hand_over,
        out_shape=tuple(jax.ShapeDtypeStruct(r.shape, r.dtype) for r in results),
        in_specs=[hbm, hbm, hbm],
        out_specs=(hbm, hbm, hbm),
        scratch_shapes=[pltpu.VMEM(r.shape, r.dtype) for r in results] + [pltpu.SemaphoreType.DMA((20,))],
        compiler_params=pltpu.CompilerParams(vmem_limit_bytes=62 * 2**20),
    )(*results)


def hand_over(big, left, newb, big_out, left_out, newb_out, big_v, left_v, newb_v, sems):
    size = big.shape[0] // 8
    parts = [(big.at[pl.ds(size * i, size)], big_v.at[pl.ds(size * i, size)], big_out.at[pl.ds(size * i, size)])
             for i in range(8)]
    parts += [(left, left_v, left_out), (newb, newb_v, newb_out)]
    reads = [pltpu.make_async_copy(src, mid, sems.at[i]) for i, (src, mid, _) in enumerate(parts)]
    writes = [pltpu.make_async_copy(mid, dst, sems.at[10 + i]) for i, (_, mid, dst) in enumerate(parts)]
    for copy in reads:
        copy.start()
    for read, write in zip(reads, writes):
        read.wait()
        write.start()
    for write in writes:
        write.wait()


def solution(mesh):
    dims = (4, 4, 8)
    placed = (P("fsdp", "tensor"), P("fsdp", "tensor"), P("tensor", None))
    return jax.shard_map(
        functools.partial(body, dims),
        mesh=mesh,
        in_specs=placed,
        out_specs=(P("fsdp", "tensor"), P(("fsdp", "tensor"), None), P("tensor", None)),
        check_vma=False,
    )
```

```python
import functools

import jax
import jax.numpy as jnp
from jax import lax
from jax.experimental import pallas as pl
from jax.experimental.pallas import tpu as pltpu
from jax.sharding import PartitionSpec as P

mu_value = 0.95
eps_value = 1e-06
f32 = jnp.float32
bf16 = jnp.bfloat16
MESH = pl.DeviceIdType.MESH
HIGHEST = lax.Precision.HIGHEST
NB = 128

KINDS = ('C', 'A2', 'C', 'C')
PLAN = (
    "p0", "p1", "p2", "p3", "p0", "p1", "p2", "p3", "p0", "p0", "w0", "p1", "p2", "p1", "ga", "w1",
    "p2", "p3", "w2", "w0", "p3", "gb", "ga", "w3", "w1", "w2", "w0", "gb", "ga", "w1", "w3", "w0",
    "w2", "ga", "gb", "ga", "w3", "f", "f", "w1", "f", "f", "w0", "f", "f", "w2", "f", "f", "f",
    "gb", "f", "w3", "f", "f", "f", "gb", "w1", "f", "w0", "f", "w2", "f", "f", "f", "f", "w3", "f",
    "f", "w1", "f", "w0", "f", "f", "f", "f", "w2", "f", "f", "l", "f", "f", "l", "w3", "f", "w1",
    "f", "l", "f", "f", "l", "f", "w2", "f", "l", "w3",
)


def dot(left, right, dims=((1,), (0,)), precision=None):
    return lax.dot_general(left, right, (dims, ((), ())), precision=precision, preferred_element_type=f32)


def exact_dot(left, right, dims=((1,), (0,))):
    return dot(left, right, dims, HIGHEST)


def split2(value):
    high = value.astype(bf16)
    return high, (value - high.astype(f32)).astype(bf16)


def dot3(left, right, dims=((1,), (0,))):
    left_high, left_low = left
    right_high, right_low = right
    return dot(left_high, right_high, dims) + (dot(left_low, right_high, dims) + dot(left_high, right_low, dims))


def factor_groups(work, inverse, first, last):
    for group in range(first, last):
        r0 = 8 * group
        n = NB - r0
        cols = [jnp.broadcast_to(work[r0:NB, r0 + j : r0 + j + 1], (n, 128)) for j in range(8)]
        top = work[r0 : r0 + 8, :]
        rows = []
        for k in range(8):
            inv = lax.rsqrt(cols[k][k : k + 1, :])
            c = cols[k] * inv
            cols[k] = c
            for j in range(k + 1, 8):
                cols[j] = cols[j] - c * c[j : j + 1, :]
            row = top[k : k + 1, :] * jnp.concatenate([inv, inv], axis=1)
            rows.append(row)
            if k < 7:
                top = top - jnp.concatenate([c[0:8], c[0:8]], axis=1) * row
            inverse[r0 + k : r0 + k + 1, :] = row[:, 128:]
        if n > 8:
            for half in (slice(0, 128), slice(128, 256)):
                rest = work[r0 + 8 : NB, half]
                for k in range(8):
                    rest = rest - cols[k][8:] * rows[k][:, half]
                work[r0 + 8 : NB, half] = rest


class Links:
    def __init__(self, dims, send_sems, recv_sems):
        self.nx, self.ny, self.nz = dims
        f, t = lax.axis_index("fsdp"), lax.axis_index("tensor")
        self.y, self.z = f // self.nz, lax.rem(f, self.nz)
        self.x, self.c = t // 2, lax.rem(t, 2)
        self.t, self.f = t, f
        self.send_sems, self.recv_sems = send_sems, recv_sems
        self.count = 0
        self.sent = []

    def size(self, axis):
        return {"x": self.nx, "y": self.ny, "z": self.nz}[axis]

    def pos(self, axis):
        return {"x": self.x, "y": self.y, "z": self.z}[axis]

    def at(self, axis, offset):
        n = self.size(axis)
        return lax.rem(self.pos(axis) + (offset % n), n)

    def device(self, dx=0, dy=0, dz=0, core=0):
        x, y, z = self.at("x", dx), self.at("y", dy), self.at("z", dz)
        c = 1 - self.c if core else self.c
        return (y * self.nz + z, x * 2 + c)

    def along(self, axis, offset):
        return self.device(**{"d" + axis: offset})

    def send(self, src, dst, device):
        number = self.count
        self.count += 1
        copy = pltpu.make_async_remote_copy(
            src_ref=src,
            dst_ref=dst,
            send_sem=self.send_sems.at[number],
            recv_sem=self.recv_sems.at[number],
            device_id=device,
            device_id_type=MESH,
        )
        copy.start()
        self.sent.append(copy)
        return number

    def wait(self, number, landing):
        pltpu.make_async_remote_copy(
            src_ref=landing,
            dst_ref=landing,
            send_sem=self.send_sems.at[number],
            recv_sem=self.recv_sems.at[number],
            device_id=self.device(core=1),
            device_id_type=MESH,
        ).wait_recv()


def cut(view):
    size = view.shape[0]
    return view.at[0 : size // 2], view.at[size // 2 : size]


def reduce_ring(links, axis, block, plus, minus):
    half = links.size(axis) // 2
    state = {}

    def add(target, slot, number):
        links.wait(number, slot)
        target[...] = target[...] + slot[...]

    def step(s):
        k = half + 1 - s
        ahead, behind = block(links.at(axis, k)), block(links.at(axis, -k))
        if s > 1:
            target, slot = (cut(ahead)[0], cut(plus.at[s - 2])[0]) if s == 2 else (ahead, plus.at[s - 2])
            add(target, slot, state["plus"])
        src, dst = (cut(ahead)[0], cut(plus.at[s - 1])[0]) if s == 1 else (ahead, plus.at[s - 1])
        state["plus"] = links.send(src, dst, links.along(axis, 1))
        if s > 1:
            target, slot = (cut(behind)[1], cut(minus.at[s - 2])[1]) if s == 2 else (behind, minus.at[s - 2])
            add(target, slot, state["minus"])
        src, dst = (cut(behind)[1], cut(minus.at[s - 1])[1]) if s == 1 else (behind, minus.at[s - 1])
        state["minus"] = links.send(src, dst, links.along(axis, -1))

    def last():
        own = block(links.pos(axis))
        target, slot = (cut(own)[0], cut(plus.at[0])[0]) if half == 1 else (own, plus.at[half - 1])
        add(target, slot, state["plus"])
        target, slot = (cut(own)[1], cut(minus.at[0])[1]) if half == 1 else (own, minus.at[half - 1])
        add(target, slot, state["minus"])

    return [functools.partial(step, s) for s in range(1, half + 1)] + [last]


def gather_ring(links, axis, block, on_block=None):
    n = links.size(axis)
    half = n // 2
    state = {}

    def step(s):
        ahead, behind = block(links.at(axis, 1 - s)), block(links.at(axis, s - 1))
        if s > 1:
            links.wait(state["plus"], ahead)
        view = cut(ahead)[0] if s == half else ahead
        state["plus"] = links.send(view, view, links.along(axis, 1))
        if s > 1:
            links.wait(state["minus"], behind)
        view = cut(behind)[1] if s == half else behind
        state["minus"] = links.send(view, view, links.along(axis, -1))
        if on_block is not None:
            on_block(links.at(axis, 1 - s))
            if s > 1:
                on_block(links.at(axis, s - 1))

    def last():
        far = cut(block(links.at(axis, half)))
        links.wait(state["plus"], far[0])
        links.wait(state["minus"], far[1])
        if on_block is not None:
            on_block(links.at(axis, half))

    return [functools.partial(step, s) for s in range(1, half + 1)] + [last]


def scatter_direct(links, axis, block, slots, stride=1):
    offsets = range(stride, links.size(axis), stride)
    numbers = []

    def send():
        for i, d in enumerate(offsets):
            numbers.append(links.send(block(links.at(axis, d)), slots.at[i], links.along(axis, d)))

    def add():
        own = block(links.pos(axis))
        total = own[...]
        for i, number in enumerate(numbers):
            links.wait(number, slots.at[i])
            total = total + slots[i]
        own[...] = total

    return send, add


def gather_direct(links, axis, block, on_block=None, stride=1):
    offsets = range(stride, links.size(axis), stride)
    numbers = []

    def send():
        own = block(links.pos(axis))
        for d in offsets:
            numbers.append(links.send(own, own, links.along(axis, d)))
        if on_block is not None:
            on_block(links.pos(axis))

    def wait():
        for d, number in zip(offsets, numbers):
            links.wait(number, block(links.at(axis, -d)))
            if on_block is not None:
                on_block(links.at(axis, -d))

    return send, wait


def chain(*steps):
    def run():
        for step in steps:
            step()

    return run


def kernel(
    dims,
    mom_hbm, grad_hbm, basis_hbm,
    out_hbm, left_hbm, newb_hbm,
    blend, grad, basis, blend_hi, blend_lo, part, from_core, x_slots,
    full, flip, flip_hi, flip_lo,
    piece_a, from_y_a, from_z_a, gram_a, piece_b, from_y_b, from_z_b, gram_b, sym, low, work, diag_inv, inverse,
    wide, y_slots, y_plus, y_minus, z_slots, pair_slots, wide_all,
    coef_wide, coef_t, coef, squares, left_bf, left_own, newb,
    load_sems, store_sems, send_sems, recv_sems,
):
    nx, ny, nz = dims
    nt = 2 * nx
    rows, width = blend.shape
    rank = basis.shape[1]
    chunk = rank // 4
    share = rows // nt
    links = Links(dims, send_sems, recv_sems)
    chip_rows = 2 * share

    loads = []
    basis_copy = pltpu.make_async_copy(basis_hbm, basis, load_sems.at[2 * nx])
    basis_copy.start()
    for k in range(nx):
        chip = links.at("x", [nx // 2, 1, nx - 1, 0][k] if nx == 4 else k + 1)
        span = pl.ds(pl.multiple_of(chip * chip_rows, chip_rows), chip_rows)
        m = pltpu.make_async_copy(mom_hbm.at[span], blend.at[span], load_sems.at[2 * k])
        g = pltpu.make_async_copy(grad_hbm.at[span], grad.at[span], load_sems.at[2 * k + 1])
        m.start()
        g.start()
        loads.append((m, g, span, chip))

    barrier = pltpu.get_barrier_semaphore()
    peers = [links.device(core=1)]
    peers += [links.device(dx=d, core=c) for d in range(1, nx) for c in (0, 1)]
    peers += [links.along("y", d) for d in range(1, ny)]
    peers += [links.along("z", d) for d in range(1, nz)]
    peers += [links.device(dx=dx, dy=dy) for dx in range(1, nx) for dy in range(1, ny)]
    for peer in peers:
        pl.semaphore_signal(barrier, inc=1, device_id=peer, device_id_type=MESH)

    def share_of(ref, chip, core):
        return ref.at[:, pl.ds(pl.multiple_of((2 * chip + core) * share, share), share)]

    def joined(*pieces):
        return jnp.concatenate(pieces, axis=1)

    basis_copy.wait()
    core_numbers = []
    for m, g, span, chip in loads:
        m.wait()
        g.wait()
        value = blend[span] + grad[span].astype(f32)
        blend[span] = value
        high = value.astype(bf16)
        rest = value - high.astype(f32)
        mid = rest.astype(bf16)
        tail = (rest - mid.astype(f32)).astype(bf16)
        blend_hi[span] = high
        blend_lo[span] = mid
        q = basis[...]
        product = dot(high, q) + (dot(mid, q) + dot(tail, q))
        for j in range(4):
            part[j, span, :] = product[:, j * chunk : (j + 1) * chunk]
        if not core_numbers:
            pl.semaphore_wait(barrier, len(peers))
        number = links.send(
            share_of(part, chip, 1 - links.c), from_core.at[:, pl.ds(chip * share, share)], links.device(core=1)
        )
        core_numbers.append((number, chip))
    for number, chip in core_numbers:
        landing = from_core.at[:, pl.ds(chip * share, share)]
        links.wait(number, landing)
        mine = share_of(part, chip, links.c)
        mine[...] = mine[...] + landing[...]

    nb = rank // NB
    fine = NB // nt

    cols = width // nz

    def rows_of(ref, row, size):
        return ref.at[:, :, pl.ds(pl.multiple_of(row, 8), size)]

    def tile_of(ref, row, size, i):
        return ref.at[lax.rem(i, 2), i // 2, pl.ds(pl.multiple_of(row, 8), size)]

    parity = lax.rem(links.z, 2)
    turn_z = 1 - 2 * parity
    pair_devices = [
        (links.y * nz + lax.rem(links.z + nz + sign * turn_z, nz), links.t) for sign in (1, -1)
    ]

    def gather_core(view):
        numbers = []

        def to_core(chip):
            numbers.append((links.send(view(chip, links.c), view(chip, links.c), links.device(core=1)), chip))

        def finish():
            for number, chip in numbers:
                links.wait(number, view(chip, 1 - links.c))

        return to_core, finish

    def project_steps(j):
        cols = slice(j * chunk, (j + 1) * chunk)

        def partial_view(chip):
            return share_of(part, chip, links.c).at[j]

        def full_view(chip, core):
            return share_of(full, chip, core).at[j]

        def keep():
            full_view(links.x, links.c)[...] = partial_view(links.x)[...]

        def turn():
            for i in range(rows // 128):
                block = full[j, 128 * i : 128 * i + 128, :].T
                flip[cols, 128 * i : 128 * i + 128] = block
                high, lower = split2(block)
                flip_hi[cols, 128 * i : 128 * i + 128] = high
                flip_lo[cols, 128 * i : 128 * i + 128] = lower

        send, add = scatter_direct(links, "x", partial_view, x_slots.at[j])
        to_core, finish = gather_core(full_view)
        share_out, wait = gather_direct(links, "x", lambda i: full_view(i, links.c), to_core)
        return [send, chain(add, keep, share_out), wait, chain(finish, turn)]

    def wide_steps(j, kind):
        base, size = j * chunk, chunk // ny
        mine = base + links.y * size
        span = slice(base, base + chunk)

        def multiply():
            for n in range(width // 256):
                part_cols = slice(256 * n, 256 * n + 256)
                values = dot3((flip_hi[span, :], flip_lo[span, :]), (blend_hi[:, part_cols], blend_lo[:, part_cols]))
                for m in range(256 // cols):
                    tile = 256 // cols * n + m
                    wide[tile % 2, tile // 2, span, :] = values[:, cols * m : cols * m + cols]

        def keep():
            tile_of(wide_all, mine, size, links.z)[...] = tile_of(wide, mine, size, links.z)[...]

        z_send, z_add = scatter_direct(links, "z", functools.partial(tile_of, wide, mine, size), z_slots.at[j])
        z_share, z_wait = gather_direct(links, "z", functools.partial(tile_of, wide_all, mine, size))
        middle = chain(z_add, keep, z_share)

        def y_block(ref, i):
            return rows_of(ref, base + i * size, size)

        if kind == "C":
            numbers = []

            def side(ref, which, h):
                return ref.at[which, :, base + h * (chunk // 2) : base + (h + 1) * (chunk // 2)]

            def pair_send():
                for h in (0, 1):
                    numbers.append(links.send(side(wide, 1 - parity, h), pair_slots.at[j, h], pair_devices[h]))

            def pair_add():
                for h in (0, 1):
                    links.wait(numbers[h], pair_slots.at[j, h])
                    mine_side = side(wide, parity, h)
                    mine_side[...] = mine_side[...] + pair_slots[j, h]

            def pair_share():
                for h in (0, 1):
                    view = side(wide_all, parity, h)
                    numbers.append(links.send(view, view, pair_devices[h]))

            def pair_wait():
                for h in (0, 1):
                    links.wait(numbers[2 + h], side(wide_all, 1 - parity, h))

            def half_block(ref, i):
                return ref.at[parity, :, pl.ds(pl.multiple_of(base + i * size, 8), size)]

            y_send, y_add = scatter_direct(links, "y", functools.partial(half_block, wide), y_slots.at[j, :, 0])
            y_share, y_wait = gather_direct(links, "y", functools.partial(half_block, wide_all))
            z_send, z_add = scatter_direct(
                links, "z", functools.partial(tile_of, wide, mine, size), z_slots.at[j], 2
            )
            z_share, z_wait = gather_direct(links, "z", functools.partial(tile_of, wide_all, mine, size), None, 2)
            return [
                chain(multiply, pair_send), chain(pair_add, y_send), chain(y_add, z_send),
                chain(z_add, keep, z_share), chain(z_wait, y_share), chain(y_wait, pair_share), pair_wait,
            ]
        if kind == "A2":
            out = reduce_ring(links, "y", functools.partial(y_block, wide), y_plus.at[j], y_minus.at[j])
            back = gather_ring(links, "y", functools.partial(y_block, wide_all))
            return (
                [chain(multiply, out[0])] + out[1:-1] + [chain(out[-1], z_send), middle, chain(z_wait, back[0])]
                + back[1:]
            )
        y_send, y_add = scatter_direct(links, "y", functools.partial(y_block, wide), y_slots.at[j])
        y_share, y_wait = gather_direct(links, "y", functools.partial(y_block, wide_all))
        return [chain(multiply, y_send), chain(y_add, z_send), middle, chain(z_wait, y_share), y_wait]

    def gram_steps(first_col, row_blocks, piece, from_y, from_z, gathered):
        y_rows = piece.shape[0] // ny
        tiles = [(i, j) for i in range(row_blocks) for j in (first_col, first_col + 1)]

        def y_part(ref, i):
            return ref.at[pl.ds(pl.multiple_of(i * y_rows, 8), y_rows)]

        gy_send, gy_add = scatter_direct(links, "y", functools.partial(y_part, piece), from_y)
        gz_send, gz_wait = gather_direct(links, "z", lambda i: from_z.at[i])
        to_core, finish = gather_core(lambda chip, core: gathered.at[2 * chip + core])
        numbers = {}

        def strip():
            picked = jnp.concatenate(
                [flip[pl.ds(pl.multiple_of(NB * i + fine * links.t, 8), fine), :] for i in range(row_blocks)], axis=0
            )
            values = exact_dot(picked, joined(full[first_col], full[first_col + 1]))
            for b, (i, j) in enumerate(tiles):
                c = NB * (j - first_col)
                piece[b * fine : b * fine + fine, :] = values[i * fine : i * fine + fine, c : c + NB]
            gy_send()

        def along_z():
            gy_add()
            from_z[links.z] = y_part(piece, links.y)[...]
            gz_send()

        def along_xy():
            gz_wait()
            total = from_z[0]
            for i in range(1, nz):
                total = total + from_z[i]
            mine = y_part(gathered.at[links.t], links.y)
            mine[...] = total
            for dx in range(nx):
                for dy in range(ny):
                    if dx or dy:
                        numbers[dx, dy] = links.send(mine, mine, links.device(dx=dx, dy=dy))

        def wait_xy():
            for dx in range(nx):
                chip = links.at("x", -dx)
                for dy in range(ny):
                    if dx or dy:
                        links.wait(numbers[dx, dy], y_part(gathered.at[2 * chip + links.c], links.at("y", -dy)))
                to_core(chip)

        def assemble():
            finish()
            for b, (i, j) in enumerate(tiles):
                for s in range(nt):
                    sym[NB * i + fine * s : NB * i + fine * s + fine, NB * j : NB * j + NB] = gathered[
                        s, b * fine : b * fine + fine, :
                    ]

        return [strip, along_z, along_xy, wait_xy, assemble]

    def factor():
        eye = jnp.where(
            lax.broadcasted_iota(jnp.int32, (NB, NB), 0) == lax.broadcasted_iota(jnp.int32, (NB, NB), 1), 1.0, 0.0
        ).astype(f32)
        inverse[...] = jnp.zeros_like(inverse)
        low[...] = jnp.zeros_like(low)
        top, rest = slice(0, 2 * NB), slice(2 * NB, rank)
        for k in range(nb):
            s = slice(NB * k, NB * k + NB)
            if k == 2:
                upper = exact_dot(inverse[top, top], sym[top, rest])
                sym[rest, rest] -= exact_dot(upper, upper, ((0,), (0,)))
                low[rest, top] = -exact_dot(upper, inverse[top, top], ((0,), (0,)))
            work[:, :NB] = sym[s, s]
            work[:, NB:] = eye
            for g in range(0, 16, 2):
                factor_groups(work, diag_inv, g, g + 2)
                yield
            block_inv = diag_inv[...]
            inverse[s, s] = block_inv
            if k:
                inverse[s, 0 : NB * k] = exact_dot(block_inv, low[s, 0 : NB * k])
            if k % 2 == 0:
                after = slice(NB * k + NB, NB * k + 2 * NB)
                upper = exact_dot(block_inv, sym[s, after])
                sym[after, after] -= exact_dot(upper, upper, ((0,), (0,)))
                low[after, 0 : NB * k + NB] -= exact_dot(upper, inverse[s, 0 : NB * k + NB], ((0,), (0,)))
            yield

    stores = []

    def left_columns(first, last, k):
        span, cols_out = slice(k * chip_rows, (k + 1) * chip_rows), slice(first, last)
        values = split2(joined(*[full[j, span, :] for j in range(last // chunk)]))
        left_bf[span, cols_out] = dot3(values, split2(inverse[cols_out, 0:last]), ((1,), (1,))).astype(bf16)

    def left_last():
        for k in range(nx):
            left_columns(3 * NB, rank, k)

    def left_rows():
        mine = share_of(full, links.x, links.c)
        left_own[...] = exact_dot(joined(*[mine[j] for j in range(4)]), inverse[...], ((1,), (1,)))
        copy = pltpu.make_async_copy(left_own, left_hbm, store_sems.at[0])
        copy.start()
        stores.append(copy)

    work_lists = {
        "ga": gram_steps(0, nb // 2, piece_a, from_y_a, from_z_a, gram_a),
        "gb": gram_steps(nb // 2, nb, piece_b, from_y_b, from_z_b, gram_b),
        "l": [functools.partial(left_columns, 0, 3 * NB, k) for k in range(nx)] + [left_last],
        "f": factor(),
    }
    for j in range(4):
        work_lists["p%d" % j] = project_steps(j)
        work_lists["w%d" % j] = wide_steps(j, KINDS[j])
    for name in PLAN:
        if name == "f":
            next(work_lists["f"])
        else:
            work_lists[name].pop(0)()
    assert not any(work_lists[name] for name in work_lists if name != "f")
    assert next(work_lists["f"], None) is None
    inverse_parts = split2(inverse[...])
    square_sum = jnp.zeros((rank, cols), f32)
    for j in range(width // 256):
        wide_cols = joined(*[wide_all[i % 2, i // 2] for i in range(256 // cols * j, 256 // cols * (j + 1))])
        block = dot3(inverse_parts, split2(wide_cols))
        out_cols = slice(256 * j, 256 * j + 256)
        coef_wide[:, out_cols] = block
        coef_t[:, out_cols] = ((mu_value - 1.0) * block).astype(bf16)
        for m in range(256 // cols):
            tile = block[:, m * cols : (m + 1) * cols]
            square_sum = square_sum + tile * tile
    mine = squares.at[links.t]
    for r in range(nb):
        span = slice(NB * r, NB * r + NB)
        mine[:, span] = jnp.broadcast_to(jnp.sum(square_sum[span, :].T, axis=0, keepdims=True), (8, NB))
    numbers = []
    for d in range(nx):
        for core in (0, 1):
            if d or core:
                other = 2 * links.at("x", -d) + (1 - links.c if core else links.c)
                numbers.append((links.send(mine, mine, links.device(dx=d, core=core)), other))
    for k in range(nx):
        span = slice(k * chip_rows, (k + 1) * chip_rows)
        blend[span] = blend[span] + dot(left_bf[span], coef_t[...])
        copy = pltpu.make_async_copy(blend.at[span], out_hbm.at[span], store_sems.at[1 + k])
        copy.start()
        stores.append(copy)
    left_rows()
    for j in range(width // 128):
        for r in range(nb):
            coef[128 * j : 128 * j + 128, NB * r : NB * r + NB] = coef_wide[
                NB * r : NB * r + NB, 128 * j : 128 * j + 128
            ].T
    for number, other in numbers:
        links.wait(number, squares.at[other])
    total = squares[0]
    for i in range(1, nt):
        total = total + squares[i]
    scale = 1.0 / jnp.sqrt(total[0:1, :] + eps_value)
    newb[...] = (coef[...] * scale).astype(bf16)
    newb_copy = pltpu.make_async_copy(newb, newb_hbm, store_sems.at[1 + nx])
    newb_copy.start()
    for copy in links.sent:
        copy.wait_send()
    for copy in stores:
        copy.wait()
    newb_copy.wait()


def body(dims, momentum, gradient, basis):
    nx, ny, nz = dims
    nt = 2 * nx
    rows, width = momentum.shape
    rank = basis.shape[1]
    share = rows // nt
    chunk = rank // 4
    fine = NB // nt
    v = pltpu.VMEM

    def gram_scratch(size):
        return (
            v((size, NB), f32), v((ny - 1, size // ny, NB), f32), v((nz, size // ny, NB), f32), v((nt, size, NB), f32)
        )

    scratch = [
        v((rows, width), f32), v((rows, width), bf16), v((width, rank), bf16),
        v((rows, width), bf16), v((rows, width), bf16),
        v((4, rows, chunk), f32), v((4, rows // 2, chunk), f32),
        v((4, nx - 1, share, rank // 4), f32),
        v((4, rows, chunk), f32),
        v((rank, rows), f32), v((rank, rows), bf16), v((rank, rows), bf16),
        *gram_scratch(4 * fine), *gram_scratch(8 * fine),
        v((rank, rank), f32), v((rank, rank), f32), v((NB, 2 * NB), f32), v((NB, NB), f32), v((rank, rank), f32),
        v((2, nz // 2, rank, width // nz), f32),
        v((4, ny - 1, 2, nz // 2, chunk // ny, width // nz), f32),
        v((4, ny // 2, 2, nz // 2, chunk // ny, width // nz), f32),
        v((4, ny // 2, 2, nz // 2, chunk // ny, width // nz), f32),
        v((4, nz - 1, chunk // ny, width // nz), f32), v((4, 2, nz // 2, chunk // 2, width // nz), f32),
        v((2, nz // 2, rank, width // nz), f32),
        v((rank, width), f32), v((rank, width), bf16), v((width, rank), f32), v((nt, 8, rank), f32),
        v((rows, rank), bf16), v((share, rank), f32), v((width, rank), bf16),
        pltpu.SemaphoreType.DMA((2 * nx + 1,)), pltpu.SemaphoreType.DMA((nx + 2,)),
        pltpu.SemaphoreType.DMA((224,)), pltpu.SemaphoreType.DMA((224,)),
    ]
    hbm = pl.BlockSpec(memory_space=pl.ANY)
    results = pl.pallas_call(
        functools.partial(kernel, dims),
        out_shape=(
            jax.ShapeDtypeStruct((rows, width), f32),
            jax.ShapeDtypeStruct((share, rank), f32),
            jax.ShapeDtypeStruct((width, rank), bf16),
        ),
        in_specs=[hbm, hbm, hbm],
        out_specs=(hbm, hbm, hbm),
        scratch_shapes=scratch,
        compiler_params=pltpu.CompilerParams(
            collective_id=0, has_side_effects=True, vmem_limit_bytes=58 * 2**20
        ),
    )(momentum, gradient, basis)
    return pl.pallas_call(
        hand_over,
        out_shape=tuple(jax.ShapeDtypeStruct(r.shape, r.dtype) for r in results),
        in_specs=[hbm, hbm, hbm],
        out_specs=(hbm, hbm, hbm),
        scratch_shapes=[pltpu.VMEM(r.shape, r.dtype) for r in results] + [pltpu.SemaphoreType.DMA((20,))],
        compiler_params=pltpu.CompilerParams(vmem_limit_bytes=62 * 2**20),
    )(*results)


def hand_over(big, left, newb, big_out, left_out, newb_out, big_v, left_v, newb_v, sems):
    size = big.shape[0] // 8
    parts = [(big.at[pl.ds(size * i, size)], big_v.at[pl.ds(size * i, size)], big_out.at[pl.ds(size * i, size)])
             for i in range(8)]
    parts += [(left, left_v, left_out), (newb, newb_v, newb_out)]
    reads = [pltpu.make_async_copy(src, mid, sems.at[i]) for i, (src, mid, _) in enumerate(parts)]
    writes = [pltpu.make_async_copy(mid, dst, sems.at[10 + i]) for i, (_, mid, dst) in enumerate(parts)]
    for copy in reads:
        copy.start()
    for read, write in zip(reads, writes):
        read.wait()
        write.start()
    for write in writes:
        write.wait()


def solution(mesh):
    dims = (4, 4, 8)
    placed = (P("fsdp", "tensor"), P("fsdp", "tensor"), P("tensor", None))
    return jax.shard_map(
        functools.partial(body, dims),
        mesh=mesh,
        in_specs=placed,
        out_specs=(P("fsdp", "tensor"), P(("fsdp", "tensor"), None), P("tensor", None)),
        check_vma=False,
    )
```

```python
import functools

import jax
import jax.numpy as jnp
from jax import lax
from jax.experimental import pallas as pl
from jax.experimental.pallas import tpu as pltpu
from jax.sharding import PartitionSpec as P

mu_value = 0.95
eps_value = 1e-06
f32 = jnp.float32
bf16 = jnp.bfloat16
MESH = pl.DeviceIdType.MESH
HIGHEST = lax.Precision.HIGHEST
NB = 128

KINDS = ('C', 'A2', 'C', 'C')
PLAN = (
    "p0", "p1", "p2", "p3", "p0", "p1", "p2", "p3", "p0", "p0", "w0", "p1", "p2", "p1", "ga", "w1",
    "p2", "p3", "w2", "w0", "p3", "gb", "ga", "w3", "w1", "w2", "w0", "gb", "ga", "w1", "w3", "w0",
    "w2", "ga", "gb", "ga", "w3", "f", "f", "w1", "f", "f", "w0", "f", "f", "w2", "f", "f", "f",
    "gb", "f", "w3", "f", "f", "f", "gb", "w1", "f", "w0", "f", "w2", "f", "f", "f", "f", "w3", "f",
    "f", "w1", "f", "w0", "f", "f", "f", "f", "w2", "f", "f", "l", "f", "f", "l", "w3", "f", "w1",
    "f", "l", "f", "f", "l", "f", "w2", "f", "l", "w3",
)


def dot(left, right, dims=((1,), (0,)), precision=None):
    return lax.dot_general(left, right, (dims, ((), ())), precision=precision, preferred_element_type=f32)


def exact_dot(left, right, dims=((1,), (0,))):
    return dot(left, right, dims, HIGHEST)


def split2(value):
    high = value.astype(bf16)
    return high, (value - high.astype(f32)).astype(bf16)


def dot3(left, right, dims=((1,), (0,))):
    left_high, left_low = left
    right_high, right_low = right
    return dot(left_high, right_high, dims) + (dot(left_low, right_high, dims) + dot(left_high, right_low, dims))


def factor_groups(work, inverse, first, last):
    for group in range(first, last):
        r0 = 8 * group
        n = NB - r0
        cols = [jnp.broadcast_to(work[r0:NB, r0 + j : r0 + j + 1], (n, 128)) for j in range(8)]
        top = work[r0 : r0 + 8, :]
        rows = []
        for k in range(8):
            inv = lax.rsqrt(cols[k][k : k + 1, :])
            c = cols[k] * inv
            cols[k] = c
            for j in range(k + 1, 8):
                cols[j] = cols[j] - c * c[j : j + 1, :]
            row = top[k : k + 1, :] * jnp.concatenate([inv, inv], axis=1)
            rows.append(row)
            if k < 7:
                top = top - jnp.concatenate([c[0:8], c[0:8]], axis=1) * row
            inverse[r0 + k : r0 + k + 1, :] = row[:, 128:]
        if n > 8:
            for half in (slice(0, 128), slice(128, 256)):
                rest = work[r0 + 8 : NB, half]
                for k in range(8):
                    rest = rest - cols[k][8:] * rows[k][:, half]
                work[r0 + 8 : NB, half] = rest


class Links:
    def __init__(self, dims, send_sems, recv_sems):
        self.nx, self.ny, self.nz = dims
        f, t = lax.axis_index("fsdp"), lax.axis_index("tensor")
        self.y, self.z = f // self.nz, lax.rem(f, self.nz)
        self.x, self.c = t // 2, lax.rem(t, 2)
        self.t, self.f = t, f
        self.send_sems, self.recv_sems = send_sems, recv_sems
        self.count = 0
        self.sent = []

    def size(self, axis):
        return {"x": self.nx, "y": self.ny, "z": self.nz}[axis]

    def pos(self, axis):
        return {"x": self.x, "y": self.y, "z": self.z}[axis]

    def at(self, axis, offset):
        n = self.size(axis)
        return lax.rem(self.pos(axis) + (offset % n), n)

    def device(self, dx=0, dy=0, dz=0, core=0):
        x, y, z = self.at("x", dx), self.at("y", dy), self.at("z", dz)
        c = 1 - self.c if core else self.c
        return (y * self.nz + z, x * 2 + c)

    def along(self, axis, offset):
        return self.device(**{"d" + axis: offset})

    def send(self, src, dst, device):
        number = self.count
        self.count += 1
        copy = pltpu.make_async_remote_copy(
            src_ref=src,
            dst_ref=dst,
            send_sem=self.send_sems.at[number],
            recv_sem=self.recv_sems.at[number],
            device_id=device,
            device_id_type=MESH,
        )
        copy.start()
        self.sent.append(copy)
        return number

    def wait(self, number, landing):
        pltpu.make_async_remote_copy(
            src_ref=landing,
            dst_ref=landing,
            send_sem=self.send_sems.at[number],
            recv_sem=self.recv_sems.at[number],
            device_id=self.device(core=1),
            device_id_type=MESH,
        ).wait_recv()


def cut(view):
    size = view.shape[0]
    return view.at[0 : size // 2], view.at[size // 2 : size]


def reduce_ring(links, axis, block, plus, minus):
    half = links.size(axis) // 2
    state = {}

    def add(target, slot, number):
        links.wait(number, slot)
        target[...] = target[...] + slot[...]

    def step(s):
        k = half + 1 - s
        ahead, behind = block(links.at(axis, k)), block(links.at(axis, -k))
        if s > 1:
            target, slot = (cut(ahead)[0], cut(plus.at[s - 2])[0]) if s == 2 else (ahead, plus.at[s - 2])
            add(target, slot, state["plus"])
        src, dst = (cut(ahead)[0], cut(plus.at[s - 1])[0]) if s == 1 else (ahead, plus.at[s - 1])
        state["plus"] = links.send(src, dst, links.along(axis, 1))
        if s > 1:
            target, slot = (cut(behind)[1], cut(minus.at[s - 2])[1]) if s == 2 else (behind, minus.at[s - 2])
            add(target, slot, state["minus"])
        src, dst = (cut(behind)[1], cut(minus.at[s - 1])[1]) if s == 1 else (behind, minus.at[s - 1])
        state["minus"] = links.send(src, dst, links.along(axis, -1))

    def last():
        own = block(links.pos(axis))
        target, slot = (cut(own)[0], cut(plus.at[0])[0]) if half == 1 else (own, plus.at[half - 1])
        add(target, slot, state["plus"])
        target, slot = (cut(own)[1], cut(minus.at[0])[1]) if half == 1 else (own, minus.at[half - 1])
        add(target, slot, state["minus"])

    return [functools.partial(step, s) for s in range(1, half + 1)] + [last]


def gather_ring(links, axis, block, on_block=None):
    n = links.size(axis)
    half = n // 2
    state = {}

    def step(s):
        ahead, behind = block(links.at(axis, 1 - s)), block(links.at(axis, s - 1))
        if s > 1:
            links.wait(state["plus"], ahead)
        view = cut(ahead)[0] if s == half else ahead
        state["plus"] = links.send(view, view, links.along(axis, 1))
        if s > 1:
            links.wait(state["minus"], behind)
        view = cut(behind)[1] if s == half else behind
        state["minus"] = links.send(view, view, links.along(axis, -1))
        if on_block is not None:
            on_block(links.at(axis, 1 - s))
            if s > 1:
                on_block(links.at(axis, s - 1))

    def last():
        far = cut(block(links.at(axis, half)))
        links.wait(state["plus"], far[0])
        links.wait(state["minus"], far[1])
        if on_block is not None:
            on_block(links.at(axis, half))

    return [functools.partial(step, s) for s in range(1, half + 1)] + [last]


def scatter_direct(links, axis, block, slots, stride=1):
    offsets = range(stride, links.size(axis), stride)
    numbers = {}

    def send(only=None):
        for i, d in enumerate(offsets):
            if d not in numbers and only in (None, d):
                numbers[d] = links.send(block(links.at(axis, d)), slots.at[i], links.along(axis, d))

    def add():
        own = block(links.pos(axis))
        total = own[...]
        for i, d in enumerate(offsets):
            links.wait(numbers[d], slots.at[i])
            total = total + slots[i]
        own[...] = total

    return send, add


def gather_direct(links, axis, block, on_block=None, stride=1):
    offsets = range(stride, links.size(axis), stride)
    numbers = []

    def send():
        own = block(links.pos(axis))
        for d in offsets:
            numbers.append(links.send(own, own, links.along(axis, d)))
        if on_block is not None:
            on_block(links.pos(axis))

    def wait():
        for d, number in zip(offsets, numbers):
            links.wait(number, block(links.at(axis, -d)))
            if on_block is not None:
                on_block(links.at(axis, -d))

    return send, wait


def chain(*steps):
    def run():
        for step in steps:
            step()

    return run


def kernel(
    dims,
    mom_hbm, grad_hbm, basis_hbm,
    out_hbm, left_hbm, newb_hbm,
    blend, grad, basis, blend_hi, blend_lo, part, from_core, x_slots,
    full, flip, flip_hi, flip_lo,
    piece_a, from_y_a, from_z_a, gram_a, piece_b, from_y_b, from_z_b, gram_b, sym, low, work, diag_inv, inverse,
    wide, y_slots, y_plus, y_minus, z_slots, pair_slots, wide_all,
    coef_wide, coef_t, coef, squares, left_bf, left_own, newb,
    load_sems, store_sems, send_sems, recv_sems,
):
    nx, ny, nz = dims
    nt = 2 * nx
    rows, width = blend.shape
    rank = basis.shape[1]
    chunk = rank // 4
    share = rows // nt
    links = Links(dims, send_sems, recv_sems)
    chip_rows = 2 * share

    loads = []
    basis_copy = pltpu.make_async_copy(basis_hbm, basis, load_sems.at[2 * nx])
    basis_copy.start()
    for k in range(nx):
        chip = links.at("x", [nx // 2, 1, nx - 1, 0][k] if nx == 4 else k + 1)
        span = pl.ds(pl.multiple_of(chip * chip_rows, chip_rows), chip_rows)
        m = pltpu.make_async_copy(mom_hbm.at[span], blend.at[span], load_sems.at[2 * k])
        g = pltpu.make_async_copy(grad_hbm.at[span], grad.at[span], load_sems.at[2 * k + 1])
        m.start()
        g.start()
        loads.append((m, g, span, chip))

    barrier = pltpu.get_barrier_semaphore()
    peers = [links.device(core=1)]
    peers += [links.device(dx=d, core=c) for d in range(1, nx) for c in (0, 1)]
    peers += [links.along("y", d) for d in range(1, ny)]
    peers += [links.along("z", d) for d in range(1, nz)]
    peers += [links.device(dx=dx, dy=dy) for dx in range(1, nx) for dy in range(1, ny)]
    for peer in peers:
        pl.semaphore_signal(barrier, inc=1, device_id=peer, device_id_type=MESH)

    def share_of(ref, chip, core):
        return ref.at[:, pl.ds(pl.multiple_of((2 * chip + core) * share, share), share)]

    def joined(*pieces):
        return jnp.concatenate(pieces, axis=1)

    basis_copy.wait()
    core_numbers = []
    x_sums = [
        scatter_direct(links, "x", lambda i, j=j: share_of(part, i, links.c).at[j], x_slots.at[j]) for j in range(4)
    ]

    def add_core(number, chip):
        landing = from_core.at[:, pl.ds(chip * share, share)]
        links.wait(number, landing)
        mine = share_of(part, chip, links.c)
        mine[...] = mine[...] + landing[...]

    for m, g, span, chip in loads:
        m.wait()
        g.wait()
        value = blend[span] + grad[span].astype(f32)
        blend[span] = value
        high = value.astype(bf16)
        rest = value - high.astype(f32)
        mid = rest.astype(bf16)
        tail = (rest - mid.astype(f32)).astype(bf16)
        blend_hi[span] = high
        blend_lo[span] = mid
        q = basis[...]
        product = dot(high, q) + (dot(mid, q) + dot(tail, q))
        for j in range(4):
            part[j, span, :] = product[:, j * chunk : (j + 1) * chunk]
        if not core_numbers:
            pl.semaphore_wait(barrier, len(peers))
        number = links.send(
            share_of(part, chip, 1 - links.c), from_core.at[:, pl.ds(chip * share, share)], links.device(core=1)
        )
        core_numbers.append((number, chip))
        if len(core_numbers) == 2:
            add_core(*core_numbers[0])
            for send, _ in x_sums:
                send(nx // 2)
    for number, chip in core_numbers[1:]:
        add_core(number, chip)
    nb = rank // NB
    fine = NB // nt

    cols = width // nz

    def rows_of(ref, row, size):
        return ref.at[:, :, pl.ds(pl.multiple_of(row, 8), size)]

    def tile_of(ref, row, size, i):
        return ref.at[lax.rem(i, 2), i // 2, pl.ds(pl.multiple_of(row, 8), size)]

    parity = lax.rem(links.z, 2)
    turn_z = 1 - 2 * parity
    pair_devices = [
        (links.y * nz + lax.rem(links.z + nz + sign * turn_z, nz), links.t) for sign in (1, -1)
    ]

    def gather_core(view):
        numbers = []

        def to_core(chip):
            numbers.append((links.send(view(chip, links.c), view(chip, links.c), links.device(core=1)), chip))

        def finish():
            for number, chip in numbers:
                links.wait(number, view(chip, 1 - links.c))

        return to_core, finish

    def project_steps(j):
        cols = slice(j * chunk, (j + 1) * chunk)

        def partial_view(chip):
            return share_of(part, chip, links.c).at[j]

        def full_view(chip, core):
            return share_of(full, chip, core).at[j]

        def keep():
            full_view(links.x, links.c)[...] = partial_view(links.x)[...]

        def turn():
            for i in range(rows // 128):
                block = full[j, 128 * i : 128 * i + 128, :].T
                flip[cols, 128 * i : 128 * i + 128] = block
                high, lower = split2(block)
                flip_hi[cols, 128 * i : 128 * i + 128] = high
                flip_lo[cols, 128 * i : 128 * i + 128] = lower

        send, add = x_sums[j]
        to_core, finish = gather_core(full_view)
        share_out, wait = gather_direct(links, "x", lambda i: full_view(i, links.c), to_core)
        return [send, chain(add, keep, share_out), wait, chain(finish, turn)]

    def wide_steps(j, kind):
        base, size = j * chunk, chunk // ny
        mine = base + links.y * size
        span = slice(base, base + chunk)

        def multiply():
            for n in range(width // 256):
                part_cols = slice(256 * n, 256 * n + 256)
                values = dot3((flip_hi[span, :], flip_lo[span, :]), (blend_hi[:, part_cols], blend_lo[:, part_cols]))
                for m in range(256 // cols):
                    tile = 256 // cols * n + m
                    wide[tile % 2, tile // 2, span, :] = values[:, cols * m : cols * m + cols]

        def keep():
            tile_of(wide_all, mine, size, links.z)[...] = tile_of(wide, mine, size, links.z)[...]

        z_send, z_add = scatter_direct(links, "z", functools.partial(tile_of, wide, mine, size), z_slots.at[j])
        z_share, z_wait = gather_direct(links, "z", functools.partial(tile_of, wide_all, mine, size))
        middle = chain(z_add, keep, z_share)

        def y_block(ref, i):
            return rows_of(ref, base + i * size, size)

        if kind == "C":
            numbers = []

            def side(ref, which, h):
                return ref.at[which, :, base + h * (chunk // 2) : base + (h + 1) * (chunk // 2)]

            def pair_send():
                for h in (0, 1):
                    numbers.append(links.send(side(wide, 1 - parity, h), pair_slots.at[j, h], pair_devices[h]))

            def pair_add():
                for h in (0, 1):
                    links.wait(numbers[h], pair_slots.at[j, h])
                    mine_side = side(wide, parity, h)
                    mine_side[...] = mine_side[...] + pair_slots[j, h]

            def pair_share():
                for h in (0, 1):
                    view = side(wide_all, parity, h)
                    numbers.append(links.send(view, view, pair_devices[h]))

            def pair_wait():
                for h in (0, 1):
                    links.wait(numbers[2 + h], side(wide_all, 1 - parity, h))

            def half_block(ref, i):
                return ref.at[parity, :, pl.ds(pl.multiple_of(base + i * size, 8), size)]

            y_send, y_add = scatter_direct(links, "y", functools.partial(half_block, wide), y_slots.at[j, :, 0])
            y_share, y_wait = gather_direct(links, "y", functools.partial(half_block, wide_all))
            z_send, z_add = scatter_direct(
                links, "z", functools.partial(tile_of, wide, mine, size), z_slots.at[j], 2
            )
            z_share, z_wait = gather_direct(links, "z", functools.partial(tile_of, wide_all, mine, size), None, 2)
            return [
                chain(multiply, pair_send), chain(pair_add, y_send), chain(y_add, z_send),
                chain(z_add, keep, z_share), chain(z_wait, y_share), chain(y_wait, pair_share), pair_wait,
            ]
        if kind == "A2":
            out = reduce_ring(links, "y", functools.partial(y_block, wide), y_plus.at[j], y_minus.at[j])
            back = gather_ring(links, "y", functools.partial(y_block, wide_all))
            return (
                [chain(multiply, out[0])] + out[1:-1] + [chain(out[-1], z_send), middle, chain(z_wait, back[0])]
                + back[1:]
            )
        y_send, y_add = scatter_direct(links, "y", functools.partial(y_block, wide), y_slots.at[j])
        y_share, y_wait = gather_direct(links, "y", functools.partial(y_block, wide_all))
        return [chain(multiply, y_send), chain(y_add, z_send), middle, chain(z_wait, y_share), y_wait]

    def gram_steps(first_col, row_blocks, piece, from_y, from_z, gathered):
        y_rows = piece.shape[0] // ny
        tiles = [(i, j) for i in range(row_blocks) for j in (first_col, first_col + 1)]

        def y_part(ref, i):
            return ref.at[pl.ds(pl.multiple_of(i * y_rows, 8), y_rows)]

        gy_send, gy_add = scatter_direct(links, "y", functools.partial(y_part, piece), from_y)
        gz_send, gz_wait = gather_direct(links, "z", lambda i: from_z.at[i])
        to_core, finish = gather_core(lambda chip, core: gathered.at[2 * chip + core])
        numbers = {}

        def strip():
            picked = jnp.concatenate(
                [flip[pl.ds(pl.multiple_of(NB * i + fine * links.t, 8), fine), :] for i in range(row_blocks)], axis=0
            )
            values = exact_dot(picked, joined(full[first_col], full[first_col + 1]))
            for b, (i, j) in enumerate(tiles):
                c = NB * (j - first_col)
                piece[b * fine : b * fine + fine, :] = values[i * fine : i * fine + fine, c : c + NB]
            gy_send()

        def along_z():
            gy_add()
            from_z[links.z] = y_part(piece, links.y)[...]
            gz_send()

        def along_xy():
            gz_wait()
            total = from_z[0]
            for i in range(1, nz):
                total = total + from_z[i]
            mine = y_part(gathered.at[links.t], links.y)
            mine[...] = total
            for dx in range(nx):
                for dy in range(ny):
                    if dx or dy:
                        numbers[dx, dy] = links.send(mine, mine, links.device(dx=dx, dy=dy))

        def wait_xy():
            for dx in range(nx):
                chip = links.at("x", -dx)
                for dy in range(ny):
                    if dx or dy:
                        links.wait(numbers[dx, dy], y_part(gathered.at[2 * chip + links.c], links.at("y", -dy)))
                to_core(chip)

        def assemble():
            finish()
            for b, (i, j) in enumerate(tiles):
                for s in range(nt):
                    sym[NB * i + fine * s : NB * i + fine * s + fine, NB * j : NB * j + NB] = gathered[
                        s, b * fine : b * fine + fine, :
                    ]

        return [strip, along_z, along_xy, wait_xy, assemble]

    def factor():
        eye = jnp.where(
            lax.broadcasted_iota(jnp.int32, (NB, NB), 0) == lax.broadcasted_iota(jnp.int32, (NB, NB), 1), 1.0, 0.0
        ).astype(f32)
        inverse[...] = jnp.zeros_like(inverse)
        low[...] = jnp.zeros_like(low)
        top, rest = slice(0, 2 * NB), slice(2 * NB, rank)
        for k in range(nb):
            s = slice(NB * k, NB * k + NB)
            if k == 2:
                upper = exact_dot(inverse[top, top], sym[top, rest])
                sym[rest, rest] -= exact_dot(upper, upper, ((0,), (0,)))
                low[rest, top] = -exact_dot(upper, inverse[top, top], ((0,), (0,)))
            work[:, :NB] = sym[s, s]
            work[:, NB:] = eye
            for g in range(0, 16, 2):
                factor_groups(work, diag_inv, g, g + 2)
                yield
            block_inv = diag_inv[...]
            inverse[s, s] = block_inv
            if k:
                inverse[s, 0 : NB * k] = exact_dot(block_inv, low[s, 0 : NB * k])
            if k % 2 == 0:
                after = slice(NB * k + NB, NB * k + 2 * NB)
                upper = exact_dot(block_inv, sym[s, after])
                sym[after, after] -= exact_dot(upper, upper, ((0,), (0,)))
                low[after, 0 : NB * k + NB] -= exact_dot(upper, inverse[s, 0 : NB * k + NB], ((0,), (0,)))
            yield

    stores = []

    def left_columns(first, last, k):
        span, cols_out = slice(k * chip_rows, (k + 1) * chip_rows), slice(first, last)
        values = split2(joined(*[full[j, span, :] for j in range(last // chunk)]))
        left_bf[span, cols_out] = dot3(values, split2(inverse[cols_out, 0:last]), ((1,), (1,))).astype(bf16)

    def left_last():
        for k in range(nx):
            left_columns(3 * NB, rank, k)

    def left_rows():
        mine = share_of(full, links.x, links.c)
        left_own[...] = exact_dot(joined(*[mine[j] for j in range(4)]), inverse[...], ((1,), (1,)))
        copy = pltpu.make_async_copy(left_own, left_hbm, store_sems.at[0])
        copy.start()
        stores.append(copy)

    work_lists = {
        "ga": gram_steps(0, nb // 2, piece_a, from_y_a, from_z_a, gram_a),
        "gb": gram_steps(nb // 2, nb, piece_b, from_y_b, from_z_b, gram_b),
        "l": [functools.partial(left_columns, 0, 3 * NB, k) for k in range(nx)] + [left_last],
        "f": factor(),
    }
    for j in range(4):
        work_lists["p%d" % j] = project_steps(j)
        work_lists["w%d" % j] = wide_steps(j, KINDS[j])
    for name in PLAN:
        if name == "f":
            next(work_lists["f"])
        else:
            work_lists[name].pop(0)()
    assert not any(work_lists[name] for name in work_lists if name != "f")
    assert next(work_lists["f"], None) is None
    inverse_parts = split2(inverse[...])
    square_sum = jnp.zeros((rank, cols), f32)
    for j in range(width // 256):
        wide_cols = joined(*[wide_all[i % 2, i // 2] for i in range(256 // cols * j, 256 // cols * (j + 1))])
        block = dot3(inverse_parts, split2(wide_cols))
        out_cols = slice(256 * j, 256 * j + 256)
        coef_wide[:, out_cols] = block
        coef_t[:, out_cols] = ((mu_value - 1.0) * block).astype(bf16)
        for m in range(256 // cols):
            tile = block[:, m * cols : (m + 1) * cols]
            square_sum = square_sum + tile * tile
    mine = squares.at[links.t]
    for r in range(nb):
        span = slice(NB * r, NB * r + NB)
        mine[:, span] = jnp.broadcast_to(jnp.sum(square_sum[span, :].T, axis=0, keepdims=True), (8, NB))
    numbers = []
    for d in range(nx):
        for core in (0, 1):
            if d or core:
                other = 2 * links.at("x", -d) + (1 - links.c if core else links.c)
                numbers.append((links.send(mine, mine, links.device(dx=d, core=core)), other))
    for k in range(nx):
        span = slice(k * chip_rows, (k + 1) * chip_rows)
        blend[span] = blend[span] + dot(left_bf[span], coef_t[...])
        copy = pltpu.make_async_copy(blend.at[span], out_hbm.at[span], store_sems.at[1 + k])
        copy.start()
        stores.append(copy)
    left_rows()
    for j in range(width // 128):
        for r in range(nb):
            coef[128 * j : 128 * j + 128, NB * r : NB * r + NB] = coef_wide[
                NB * r : NB * r + NB, 128 * j : 128 * j + 128
            ].T
    for number, other in numbers:
        links.wait(number, squares.at[other])
    total = squares[0]
    for i in range(1, nt):
        total = total + squares[i]
    scale = 1.0 / jnp.sqrt(total[0:1, :] + eps_value)
    newb[...] = (coef[...] * scale).astype(bf16)
    newb_copy = pltpu.make_async_copy(newb, newb_hbm, store_sems.at[1 + nx])
    newb_copy.start()
    for copy in links.sent:
        copy.wait_send()
    for copy in stores:
        copy.wait()
    newb_copy.wait()


def body(dims, momentum, gradient, basis):
    nx, ny, nz = dims
    nt = 2 * nx
    rows, width = momentum.shape
    rank = basis.shape[1]
    share = rows // nt
    chunk = rank // 4
    fine = NB // nt
    v = pltpu.VMEM

    def gram_scratch(size):
        return (
            v((size, NB), f32), v((ny - 1, size // ny, NB), f32), v((nz, size // ny, NB), f32), v((nt, size, NB), f32)
        )

    scratch = [
        v((rows, width), f32), v((rows, width), bf16), v((width, rank), bf16),
        v((rows, width), bf16), v((rows, width), bf16),
        v((4, rows, chunk), f32), v((4, rows // 2, chunk), f32),
        v((4, nx - 1, share, rank // 4), f32),
        v((4, rows, chunk), f32),
        v((rank, rows), f32), v((rank, rows), bf16), v((rank, rows), bf16),
        *gram_scratch(4 * fine), *gram_scratch(8 * fine),
        v((rank, rank), f32), v((rank, rank), f32), v((NB, 2 * NB), f32), v((NB, NB), f32), v((rank, rank), f32),
        v((2, nz // 2, rank, width // nz), f32),
        v((4, ny - 1, 2, nz // 2, chunk // ny, width // nz), f32),
        v((4, ny // 2, 2, nz // 2, chunk // ny, width // nz), f32),
        v((4, ny // 2, 2, nz // 2, chunk // ny, width // nz), f32),
        v((4, nz - 1, chunk // ny, width // nz), f32), v((4, 2, nz // 2, chunk // 2, width // nz), f32),
        v((2, nz // 2, rank, width // nz), f32),
        v((rank, width), f32), v((rank, width), bf16), v((width, rank), f32), v((nt, 8, rank), f32),
        v((rows, rank), bf16), v((share, rank), f32), v((width, rank), bf16),
        pltpu.SemaphoreType.DMA((2 * nx + 1,)), pltpu.SemaphoreType.DMA((nx + 2,)),
        pltpu.SemaphoreType.DMA((224,)), pltpu.SemaphoreType.DMA((224,)),
    ]
    hbm = pl.BlockSpec(memory_space=pl.ANY)
    results = pl.pallas_call(
        functools.partial(kernel, dims),
        out_shape=(
            jax.ShapeDtypeStruct((rows, width), f32),
            jax.ShapeDtypeStruct((share, rank), f32),
            jax.ShapeDtypeStruct((width, rank), bf16),
        ),
        in_specs=[hbm, hbm, hbm],
        out_specs=(hbm, hbm, hbm),
        scratch_shapes=scratch,
        compiler_params=pltpu.CompilerParams(
            collective_id=0, has_side_effects=True, vmem_limit_bytes=58 * 2**20
        ),
    )(momentum, gradient, basis)
    return pl.pallas_call(
        hand_over,
        out_shape=tuple(jax.ShapeDtypeStruct(r.shape, r.dtype) for r in results),
        in_specs=[hbm, hbm, hbm],
        out_specs=(hbm, hbm, hbm),
        scratch_shapes=[pltpu.VMEM(r.shape, r.dtype) for r in results] + [pltpu.SemaphoreType.DMA((20,))],
        compiler_params=pltpu.CompilerParams(vmem_limit_bytes=62 * 2**20),
    )(*results)


def hand_over(big, left, newb, big_out, left_out, newb_out, big_v, left_v, newb_v, sems):
    size = big.shape[0] // 8
    parts = [(big.at[pl.ds(size * i, size)], big_v.at[pl.ds(size * i, size)], big_out.at[pl.ds(size * i, size)])
             for i in range(8)]
    parts += [(left, left_v, left_out), (newb, newb_v, newb_out)]
    reads = [pltpu.make_async_copy(src, mid, sems.at[i]) for i, (src, mid, _) in enumerate(parts)]
    writes = [pltpu.make_async_copy(mid, dst, sems.at[10 + i]) for i, (_, mid, dst) in enumerate(parts)]
    for copy in reads:
        copy.start()
    for read, write in zip(reads, writes):
        read.wait()
        write.start()
    for write in writes:
        write.wait()


def solution(mesh):
    dims = (4, 4, 8)
    placed = (P("fsdp", "tensor"), P("fsdp", "tensor"), P("tensor", None))
    return jax.shard_map(
        functools.partial(body, dims),
        mesh=mesh,
        in_specs=placed,
        out_specs=(P("fsdp", "tensor"), P(("fsdp", "tensor"), None), P("tensor", None)),
        check_vma=False,
    )
```
